128 devices in a mesh: head: 4 (over x), outer: 8 (over y_hi, z), inner: 4 (over y_lo, core).
Axes of the slice: x: 4, y: 4 (y_hi: 2, y_lo: 2; y = y_hi * 2 + y_lo), z: 4, core: 2. Of those that a mesh axis runs over, the one named last changes fastest.
Arguments:
- queries: bfloat16 [8192, 8192], P(('outer', 'inner'), 'head')
- keys: bfloat16 [8192, 1024], P(('outer', 'inner'), 'head')
- values: bfloat16 [8192, 1024], P(('outer', 'inner'), 'head'), may hold values from -6 to 6
- positions: int32 [8192], P(('outer', 'inner')), may hold values from 0 to 8191, as said below
- residual: float32 [32, 256, 8192], P(('outer', 'inner'), 'head'), may hold values from -1.2 to 1.2
- gain: float32 [8192], replicated, may hold values from 0.1 to 1.9
Outputs:
- stream: float32 [32, 256, 8192], P(('outer', 'inner'), 'head')
- normed: bfloat16 [32, 256, 8192], P(('outer', 'inner'), 'head')
The draws below stay inside these ranges and needn't reach their ends.
Inputs may be any that keep to these rules, and one draw needn't show every extreme that they name: positions holds each of 0 to 8191 once; each aligned run of 128 rows holds consecutive positions in increasing order.
All inputs are finite; a program needn't handle non-finite values.
Results may differ from the reference program's by a relative error of at most 0.0075.
Values may be sent and summed in bfloat16 or wider, within the bound.
A program may use at most 128 MiB of HBM per device.

```python
import jax
import jax.numpy as jnp
from jax import lax

HQ = 64
KV = 8
HD = 128
TOK_DEV = 256
D = 8192
CTX = 32
TOKENS = 8192


def draw_queries(key, part):
    key = jax.random.fold_in(key, 1)
    base = 1.4 * jax.random.normal(key, (TOKENS, HQ * HD), jnp.float32)
    return base.astype(jnp.bfloat16)


def draw_keys(key, part):
    key = jax.random.fold_in(key, 2)
    base = 1.4 * jax.random.normal(key, (TOKENS, KV * HD), jnp.float32)
    return base.astype(jnp.bfloat16)


def draw_positions(key, part):
    key = jax.random.fold_in(key, 3)
    half = TOK_DEV // 2
    order = jax.random.permutation(key, 2 * CTX).astype(jnp.int32)
    rows = jnp.arange(TOKENS, dtype=jnp.int32)
    return order[rows // half] * half + rows % half


def level_of(rng, shape, shards, low, high):
    def one(position, blocks):
        steps = jax.random.uniform(jax.random.fold_in(jax.random.fold_in(rng, 6), position), (blocks,), jnp.float32, low / len(shards), high / len(shards))
        return jnp.repeat(jnp.exp(steps), shape[position] // blocks).reshape((-1,) + (1,) * (len(shape) - position - 1))

    level = one(*shards[0])
    for cut in shards[1:]:
        level = level * one(*cut)
    return level


def bell_draw(own_key, extent, width, limit, split=(), held_as=jnp.bfloat16):
    result = jax.random.normal(own_key, extent, jnp.float32) * width
    if len(split) > 0:
        result = level_of(own_key, extent, split, -0.22, 0.18) * result
    return jnp.clip(result, min=-limit, max=limit).astype(held_as)


def setup_inputs(seed: int = 0) -> dict:
    splits = jax.random.split(jax.random.key(seed), 7)
    queries = draw_queries(jax.random.fold_in(splits[6], 71), 0)
    keys = draw_keys(jax.random.fold_in(splits[6], 71), 0)
    values = bell_draw(splits[2], (TOKENS, KV * HD), 1.0, 6.0, ((0, 32), (1, 4)))
    positions = draw_positions(jax.random.fold_in(splits[6], 71), 0)
    residual = bell_draw(splits[4], (CTX, TOK_DEV, D), 0.2, 1.2, ((0, 32), (1, 4)), jnp.float32)
    gain = jnp.clip(1.0 + 0.18 * jax.random.normal(splits[5], (D,), jnp.float32), 0.1, 1.9)
    return {"queries": queries, "keys": keys, "values": values, "positions": positions, "residual": residual, "gain": gain}


def reference(queries, keys, values, positions, residual, gain):
    group = HQ // KV
    scale = 1.0 / HD ** 0.5
    allowed = positions[None, :] <= positions[:, None]

    def one_head(h):
        g = h // group
        qh = lax.dynamic_slice_in_dim(queries, (h * HD).astype(jnp.int32), HD, 1)
        kh = lax.dynamic_slice_in_dim(keys, (g * HD).astype(jnp.int32), HD, 1)
        vh = lax.dynamic_slice_in_dim(values, (g * HD).astype(jnp.int32), HD, 1)
        scores = jnp.dot(qh, kh.T, preferred_element_type=jnp.float32) * scale
        scores = jnp.where(allowed, scores, -jnp.inf)
        top = lax.optimization_barrier(jnp.max(scores, axis=1, keepdims=True))
        weights = jnp.where(allowed, jnp.exp(scores - top), 0.0)
        total = lax.optimization_barrier(jnp.sum(weights, axis=1, keepdims=True))
        out = jnp.dot(weights.astype(jnp.bfloat16), vh, preferred_element_type=jnp.float32) / total
        return out.astype(jnp.bfloat16)
    heads_out = lax.map(one_head, jnp.arange(HQ, dtype=jnp.int32))
    attended = jnp.transpose(heads_out, (1, 0, 2)).reshape(TOKENS, D)
    stream = residual + attended.astype(jnp.float32).reshape(CTX, TOK_DEV, D)
    inv = lax.rsqrt(lax.optimization_barrier(jnp.mean(stream * stream, axis=-1, keepdims=True)) + 1e-05)
    normed = (stream * inv * gain).astype(jnp.bfloat16)
    return (stream, normed)
```

```python
import jax
import jax.numpy as jnp
from jax import lax
from jax.experimental import pallas as pl
from jax.experimental.pallas import tpu as pltpu
from jax.sharding import PartitionSpec as P

HD = 128
ROWS = 256
GROUP = 8
PART = 32
TILES = 16
TILE = GROUP * PART
MSG = 2 * ROWS + 32
CHUNK = 4 * ROWS
STEPS = 8
EARLY = 5
HIDDEN = -1e30
MESH = pl.DeviceIdType.MESH

PLACES = [(0, 0), (1, 0), (3, 0), (0, 1), (0, 3), (2, 0), (0, 2),
          (1, 1), (3, 3), (1, 3), (3, 1), (2, 1), (2, 3), (1, 2), (3, 2), (2, 2)]


def dot(a, b):
    return jnp.dot(a, b, preferred_element_type=jnp.float32)


def dot_nt(a, b):
    return lax.dot_general(a, b, (((1,), (1,)), ((), ())), preferred_element_type=jnp.float32)


def forwards(place):
    out = []
    if place == 0:
        for j, (dz, dy) in enumerate(PLACES[1:7], 1):
            out += [(0, dz, dy, j), (1, dz, dy, j)]
        return out
    dz, dy = PLACES[place]
    for step in (1, 3, 2):
        if dy == 0:
            out.append((0, 0, step, PLACES.index((dz, step))))
        elif dz == 0:
            out.append((1, step, 0, PLACES.index((step, dy))))
    return out


SENDS = [(j,) + f for j in range(16) for f in forwards(j)]


def kernel(
    pos_ref, q_hbm, k_hbm, v_hbm, res_hbm, gain_ref, stream_hbm, normed_hbm,
    kv, other, bias, qraw, qx, top, acc, obuf, att, res, sbuf, nbuf,
    stage_sem, kv_send, kv_recv, q_send, q_recv, sib_send, att_send, att_recv, res_sem, out_sem,
):
    x = lax.axis_index("head")
    outer = lax.axis_index("outer")
    inner = lax.axis_index("inner")
    y_hi, z = outer // 4, lax.rem(outer, 4)
    y_lo, c = inner // 2, lax.rem(inner, 2)
    y = y_hi * 2 + y_lo
    sib = 1 - c

    def chip(dx, dz, dy, core):
        zz, yy = lax.rem(z + dz, 4), lax.rem(y + dy, 4)
        return (lax.rem(x + dx, 4), (yy // 2) * 4 + zz, lax.rem(yy, 2) * 2 + core)

    mine = pl.ds(pl.multiple_of(c * HD, HD), HD)
    theirs = pl.ds(pl.multiple_of(sib * HD, HD), HD)
    stage = [
        pltpu.make_async_copy(k_hbm.at[:, mine], kv.at[c, pl.ds(0, ROWS)], stage_sem.at[0]),
        pltpu.make_async_copy(v_hbm.at[:, mine], kv.at[c, pl.ds(ROWS, ROWS)], stage_sem.at[1]),
        pltpu.make_async_copy(k_hbm.at[:, theirs], other.at[pl.ds(0, ROWS)], stage_sem.at[2]),
        pltpu.make_async_copy(v_hbm.at[:, theirs], other.at[pl.ds(ROWS, ROWS)], stage_sem.at[3]),
    ]
    for copy in stage:
        copy.start()
    wide = GROUP * HD
    q_mine = pltpu.make_async_copy(
        q_hbm.at[:, pl.ds(pl.multiple_of(c * wide, wide), wide)], qraw.at[c], stage_sem.at[4]
    )
    q_mine.start()
    res_in = pltpu.make_async_copy(res_hbm, res, res_sem)
    res_in.start()

    partners = [chip(0, 0, 0, sib)]
    partners += [chip(0, dz, dy, c) for dz, dy in PLACES[1:7]]
    partners += [chip(dx, 0, 0, core) for dx in (1, 2, 3) for core in (c, sib)]
    barrier = pltpu.get_barrier_semaphore()
    for partner in partners:
        pl.semaphore_signal(barrier, inc=1, device_id=partner, device_id_type=MESH)

    for run in range(2):
        block = (pos_ref[run : run + 1, :] >> 7).astype(jnp.float32)
        tile = jnp.broadcast_to(block, (16, HD)).astype(jnp.bfloat16)
        kv[c, 2 * ROWS + 16 * run : 2 * ROWS + 16 * run + 16, :] = tile
        other[2 * ROWS + 16 * run : 2 * ROWS + 16 * run + 16, :] = tile
    for copy in stage:
        copy.wait()
    pl.semaphore_wait(barrier, len(partners))

    def kv_copy(index):
        place, half, dz, dy, there = SENDS[index]
        return pltpu.make_async_remote_copy(
            src_ref=kv.at[2 * place + half],
            dst_ref=kv.at[2 * there + half],
            send_sem=kv_send.at[index],
            recv_sem=kv_recv.at[2 * there + half],
            device_id=chip(0, dz, dy, c),
            device_id_type=MESH,
        )

    def first_copy(n, half):
        dz, dy = PLACES[1 + n]
        return pltpu.make_async_remote_copy(
            src_ref=kv.at[half],
            dst_ref=kv.at[2 * (1 + n) + half],
            send_sem=kv_send.at[2 * n + half],
            recv_sem=kv_recv.at[2 * (1 + n) + half],
            device_id=chip(0, dz, dy, c),
            device_id_type=MESH,
        )

    def arrival(slot):
        return pltpu.make_async_remote_copy(
            src_ref=kv.at[slot],
            dst_ref=kv.at[slot],
            send_sem=kv_send.at[0],
            recv_sem=kv_recv.at[slot],
            device_id=chip(0, 0, 0, sib),
            device_id_type=MESH,
        )

    to_sib = pltpu.make_async_remote_copy(
        src_ref=other, dst_ref=kv.at[c], send_sem=sib_send, recv_sem=kv_recv.at[c],
        device_id=chip(0, 0, 0, sib), device_id_type=MESH,
    )
    to_sib.start()
    q_out = pltpu.make_async_remote_copy(
        src_ref=q_hbm.at[:, pl.ds(pl.multiple_of(sib * wide, wide), wide)],
        dst_ref=qraw.at[c],
        send_sem=q_send,
        recv_sem=q_recv,
        device_id=chip(0, 0, 0, sib),
        device_id_type=MESH,
    )
    q_out.start()
    for n in range(4):
        first_copy(n, c).start()
    arrival(sib).wait_recv()
    for n in range(4):
        first_copy(n, sib).start()
    for n in (4, 5):
        first_copy(n, c).start()
        first_copy(n, sib).start()

    lane = lax.broadcasted_iota(jnp.int32, (16, HD), 1)
    own = jnp.zeros((16, HD), jnp.float32)
    for run in range(4):
        at = 2 * ROWS + 16 * (run % 2)
        own = jnp.where(lane == run, kv[run // 2, at : at + 16, :].astype(jnp.float32), own)

    def fill_bias(slot):
        for run in range(2):
            block = kv[slot, 2 * ROWS + 16 * run : 2 * ROWS + 16 * run + 16, :].astype(jnp.float32)
            tile = jnp.where(block < own, 0.0, HIDDEN).astype(jnp.bfloat16)
            for r in range(8):
                bias[slot, run * HD + 16 * r : run * HD + 16 * r + 16, :] = tile

    q_mine.wait()
    q_in = pltpu.make_async_remote_copy(
        src_ref=qraw.at[sib], dst_ref=qraw.at[sib], send_sem=q_send, recv_sem=q_recv,
        device_id=chip(0, 0, 0, sib), device_id_type=MESH,
    )
    q_in.wait_recv()
    scale = 1.4426950408889634 / HD**0.5
    lanes = lax.broadcasted_iota(jnp.int32, (TILE, HD), 1)
    row = lax.rem(lax.broadcasted_iota(jnp.int32, (TILE, HD), 0), PART)

    def begin(tile, carry):
        shard, part = tile // 8, lax.rem(tile, 8)
        run = part // 4
        rows = pl.ds(pl.multiple_of(part * PART, PART), PART)
        for h in range(GROUP):
            piece = qraw[shard, rows, h * HD : (h + 1) * HD].astype(jnp.float32) * scale
            qx[tile, h * PART : (h + 1) * PART, :HD] = piece.astype(jnp.bfloat16)
        qx[tile, :, HD:] = jnp.where(lanes == 2 * shard + run, 1.0, 0.0).astype(jnp.bfloat16)
        keys = pl.ds(pl.multiple_of(run * HD, HD), HD)
        vals = pl.ds(pl.multiple_of(ROWS + run * HD, HD), HD)
        s = dot_nt(qx[tile, :, :HD], kv[shard, keys, :])
        s = jnp.where(lanes <= row + lax.rem(part, 4) * PART, s, HIDDEN)
        high = jnp.broadcast_to(jnp.max(s, axis=1, keepdims=True), (TILE, HD))
        p = jnp.exp2(s - high).astype(jnp.bfloat16)
        v = kv[shard, vals, :]
        top[tile] = high
        acc[tile] = dot(p, jnp.concatenate([v, jnp.ones_like(v)], axis=1))
        return carry

    lax.fori_loop(0, TILES, begin, 0, unroll=4)

    def attend(tile, step):
        k = jnp.concatenate([kv[4 * step + a, :ROWS, :] for a in range(4)], axis=0)
        b = jnp.concatenate([bias[4 * step + a] for a in range(4)], axis=0)
        v = jnp.concatenate([kv[4 * step + a, ROWS : 2 * ROWS, :] for a in range(4)], axis=0)
        s = dot_nt(qx[tile], jnp.concatenate([k, b], axis=1))
        before = top[tile]
        high = jnp.maximum(before, jnp.max(s, axis=1, keepdims=True))
        p = jnp.exp2(s - high[:, :1]).astype(jnp.bfloat16)
        fade = jnp.exp2(before - high)
        top[tile] = high
        acc[tile] = acc[tile] * jnp.concatenate([fade, fade], axis=1) + dot(
            p, jnp.concatenate([v, jnp.ones_like(v)], axis=1)
        )

    def receive(step):
        for i in range(STEPS):

            @pl.when(step == i)
            def _():
                for place in (2 * i, 2 * i + 1):
                    if place:
                        for half in range(2):
                            arrival(2 * place + half).wait_recv()
                    for index, send in enumerate(SENDS):
                        if send[0] == place and place:
                            kv_copy(index).start()

        for a in range(4):
            fill_bias(4 * step + a)

    def early(step, carry):
        receive(step)
        for tile in range(TILES):
            attend(tile, step)
        return carry

    lax.fori_loop(0, EARLY, early, 0)

    def rest(step, carry):
        receive(step)
        return carry

    lax.fori_loop(EARLY, STEPS, rest, 0)

    def att_copy(g, dx):
        half, shard = g // 2, lax.rem(c + 1 + g, 2)
        there = lax.rem(x + dx, 4)
        tile = shard * 8 + there * 2 + half
        return tile, pltpu.make_async_remote_copy(
            src_ref=obuf.at[tile],
            dst_ref=att.at[half, 2 * x + c],
            send_sem=att_send.at[tile],
            recv_sem=att_recv.at[half, 2 * x + c],
            device_id=chip(dx, 0, 0, shard),
            device_id_type=MESH,
        )

    def finish(g, carry):
        half, shard = g // 2, lax.rem(c + 1 + g, 2)
        for step in range(EARLY, STEPS):
            for quarter in range(4):
                attend(shard * 8 + quarter * 2 + half, step)
        for quarter in range(4):
            tile = shard * 8 + quarter * 2 + half
            both = acc[tile]
            o = (both[:, :HD] / both[:, HD:]).astype(jnp.bfloat16)
            for h in range(GROUP):
                obuf[tile, :, h * HD : (h + 1) * HD] = o[h * PART : (h + 1) * PART, :]
        for dx in (1, 2, 3):
            att_copy(g, dx)[1].start()

        @pl.when(lax.rem(g, 2) == 0)
        def _():
            att_copy(g, 0)[1].start()

        @pl.when(lax.rem(g, 2) == 1)
        def _():
            att[half, 2 * x + c] = obuf[c * 8 + x * 2 + half]

        return carry

    lax.fori_loop(0, 4, finish, 0)

    def finalize(half):
        for n in range(1, 8):
            source = lax.rem(2 * x + c + n, 8)
            pltpu.make_async_remote_copy(
                src_ref=att.at[half, source], dst_ref=att.at[half, source], send_sem=q_send,
                recv_sem=att_recv.at[half, source], device_id=chip(0, 0, 0, sib), device_id_type=MESH,
            ).wait_recv()

        def rows16(i, carry):
            rows = pl.ds(pl.multiple_of(half * PART + 16 * i, 16), 16)
            local = pl.ds(pl.multiple_of(16 * i, 16), 16)
            squares = jnp.zeros((16, HD), jnp.float32)
            for source in range(8):
                cols = slice(source * wide, (source + 1) * wide)
                s = res[rows, cols] + att[half, source, local, :].astype(jnp.float32)
                sbuf[rows, cols] = s
                sq = s * s
                for a in range(8):
                    squares += sq[:, a * HD : (a + 1) * HD]
            inv = lax.rsqrt(jnp.sum(squares, axis=1, keepdims=True) * (1.0 / (8 * wide)) + 1e-05)
            for source in range(8):
                cols = slice(source * wide, (source + 1) * wide)
                nbuf[rows, cols] = (sbuf[rows, cols] * inv * gain_ref[:, cols]).astype(jnp.bfloat16)
            return carry

        lax.fori_loop(0, 2, rows16, 0)
        rows = pl.ds(half * PART, PART)
        outs = [
            pltpu.make_async_copy(sbuf.at[rows], stream_hbm.at[rows], out_sem.at[2 * half]),
            pltpu.make_async_copy(nbuf.at[rows], normed_hbm.at[rows], out_sem.at[2 * half + 1]),
        ]
        for copy in outs:
            copy.start()
        return outs

    res_in.wait()
    outs = finalize(0) + finalize(1)
    to_sib.wait_send()
    q_out.wait_send()
    for n in range(6):
        for half in range(2):
            first_copy(n, half).wait_send()
    for index in range(12, len(SENDS)):
        kv_copy(index).wait_send()

    def sent(g, carry):
        for dx in (1, 2, 3):
            att_copy(g, dx)[1].wait_send()

        @pl.when(lax.rem(g, 2) == 0)
        def _():
            att_copy(g, 0)[1].wait_send()

        return carry

    lax.fori_loop(0, 4, sent, 0)
    for copy in outs:
        copy.wait()


def per_device(queries, keys, values, positions, residual, gain):
    width = residual.shape[2]
    rows = residual.shape[1]
    hbm = pl.BlockSpec(memory_space=pl.ANY)
    vmem = pl.BlockSpec(memory_space=pltpu.VMEM)
    dma = pltpu.SemaphoreType.DMA
    bf16, f32 = jnp.bfloat16, jnp.float32
    stream, normed = pl.pallas_call(
        kernel,
        out_shape=(
            jax.ShapeDtypeStruct((rows, width), f32),
            jax.ShapeDtypeStruct((rows, width), bf16),
        ),
        in_specs=[vmem, hbm, hbm, hbm, hbm, vmem],
        out_specs=(hbm, hbm),
        scratch_shapes=[
            pltpu.VMEM((32, MSG, HD), bf16),
            pltpu.VMEM((MSG, HD), bf16),
            pltpu.VMEM((32, ROWS, HD), bf16),
            pltpu.VMEM((2, ROWS, GROUP * HD), bf16),
            pltpu.VMEM((TILES, TILE, 2 * HD), bf16),
            pltpu.VMEM((TILES, TILE, HD), f32),
            pltpu.VMEM((TILES, TILE, 2 * HD), f32),
            pltpu.VMEM((TILES, PART, GROUP * HD), bf16),
            pltpu.VMEM((2, 8, PART, GROUP * HD), bf16),
            pltpu.VMEM((rows, width), f32),
            pltpu.VMEM((rows, width), f32),
            pltpu.VMEM((rows, width), bf16),
            dma((5,)),
            dma((len(SENDS),)),
            dma((32,)),
            dma,
            dma,
            dma,
            dma((TILES,)),
            dma((2, 8)),
            dma,
            dma((4,)),
        ],
        compiler_params=pltpu.CompilerParams(
            collective_id=0, has_side_effects=True, vmem_limit_bytes=60 * 2**20
        ),
    )(
        positions.reshape(2, HD), queries, keys, values, residual[0], gain.reshape(1, width)
    )
    return (stream[None], normed[None])


def solution(mesh):
    both = ("outer", "inner")
    return jax.shard_map(
        per_device,
        mesh=mesh,
        in_specs=(P(both, "head"), P(both, "head"), P(both, "head"), P(both), P(both, "head", None), P()),
        out_specs=(P(both, "head", None), P(both, "head", None)),
        check_vma=False,
    )
```

```python
import jax
import jax.numpy as jnp
from jax import lax
from jax.experimental import pallas as pl
from jax.experimental.pallas import tpu as pltpu
from jax.sharding import PartitionSpec as P

HD = 128
ROWS = 256
GROUP = 8
PART = 32
TILES = 16
TILE = GROUP * PART
MSG = 2 * ROWS + 32
STEPS = 6
HIDDEN = -1e30
MESH = pl.DeviceIdType.MESH

PLACES = [(0, 0), (1, 0), (3, 0), (0, 1), (0, 3), (2, 0), (0, 2),
          (1, 1), (1, 3), (3, 1), (3, 3), (2, 1), (2, 3), (1, 2), (3, 2), (2, 2)]

SERVED = [(1, (1, 2, 3, 4), 1), (3, (5, 6, 7, 8), 0), (4, (9, 10), 0), (5, (5, 6, 7, 8), 1), (6, (9, 10), 1),
          (9, (11, 12, 13), 2), (10, (14,), 2)]
LAST = (13, 14, 15)
BAND = TILES // 2


def dot(a, b):
    return jnp.dot(a, b, preferred_element_type=jnp.float32)


def dot_nt(a, b):
    return lax.dot_general(a, b, (((1,), (1,)), ((), ())), preferred_element_type=jnp.float32)


def forwards(place):
    out = []
    here = PLACES[place]
    for half in range(2):
        a, b = here if half == 0 else here[::-1]
        there = []
        if a == 0 and b == 0:
            there += [(1, 0), (3, 0)]
        if a == 1 and b == 0:
            there.append((2, 0))
        if b == 0:
            there += [(a, 1), (a, 3)]
        if (b == 1 and a % 2 == 0) or (b == 3 and a % 2 == 1):
            there.append((a, 2))
        for na, nb in there:
            da, db = (na - a) % 4, (nb - b) % 4
            step, new = ((da, db), (na, nb)) if half == 0 else ((db, da), (nb, na))
            out.append((half,) + step + (PLACES.index(new),))
    return out


FIRST = forwards(0)
SENDS = [(j,) + f for j in range(16) for f in forwards(j)]
AROUND = [(1, 0), (3, 0), (0, 1), (0, 3)]


def kernel(
    pos_ref, q_hbm, k_hbm, v_hbm, att,
    kv, other, bias, qraw, qx, top, acc, obuf, s_even, s_odd, p_even, p_odd, f_even, f_odd,
    stage_sem, kv_send, kv_recv, q_send, q_recv, sib_send, att_send, att_recv, out_sem,
):
    x = lax.axis_index("head")
    outer = lax.axis_index("outer")
    inner = lax.axis_index("inner")
    y_hi, z = outer // 4, lax.rem(outer, 4)
    y_lo, c = inner // 2, lax.rem(inner, 2)
    y = y_hi * 2 + y_lo
    sib = 1 - c

    def chip(dx, dz, dy, core):
        zz, yy = lax.rem(z + dz, 4), lax.rem(y + dy, 4)
        return (lax.rem(x + dx, 4), (yy // 2) * 4 + zz, lax.rem(yy, 2) * 2 + core)

    mine = pl.ds(pl.multiple_of(c * HD, HD), HD)
    theirs = pl.ds(pl.multiple_of(sib * HD, HD), HD)
    stage = [
        pltpu.make_async_copy(k_hbm.at[:, mine], kv.at[c, pl.ds(0, ROWS)], stage_sem.at[0]),
        pltpu.make_async_copy(v_hbm.at[:, mine], kv.at[c, pl.ds(ROWS, ROWS)], stage_sem.at[1]),
        pltpu.make_async_copy(k_hbm.at[:, theirs], other.at[pl.ds(0, ROWS)], stage_sem.at[2]),
        pltpu.make_async_copy(v_hbm.at[:, theirs], other.at[pl.ds(ROWS, ROWS)], stage_sem.at[3]),
    ]
    for copy in stage:
        copy.start()
    wide = GROUP * HD
    q_mine = pltpu.make_async_copy(
        q_hbm.at[:, pl.ds(pl.multiple_of(c * wide, wide), wide)], qraw.at[c], stage_sem.at[4]
    )
    q_mine.start()

    partners = [chip(0, 0, 0, sib)]
    partners += [chip(0, dz, dy, c) for dz, dy in AROUND]
    partners += [chip(dx, 0, 0, core) for dx in (1, 2, 3) for core in (c, sib)]
    barrier = pltpu.get_barrier_semaphore()
    for partner in partners:
        pl.semaphore_signal(barrier, inc=1, device_id=partner, device_id_type=MESH)

    for run in range(2):
        block = (pos_ref[run : run + 1, :] >> 7).astype(jnp.float32)
        tile = jnp.broadcast_to(block, (16, HD)).astype(jnp.bfloat16)
        kv[c, 2 * ROWS + 16 * run : 2 * ROWS + 16 * run + 16, :] = tile
        other[2 * ROWS + 16 * run : 2 * ROWS + 16 * run + 16, :] = tile
    for copy in stage:
        copy.wait()
    pl.semaphore_wait(barrier, len(partners))

    def kv_copy(index):
        place, half, dz, dy, there = SENDS[index]
        return pltpu.make_async_remote_copy(
            src_ref=kv.at[2 * place + half],
            dst_ref=kv.at[2 * there + half],
            send_sem=kv_send.at[index],
            recv_sem=kv_recv.at[2 * there + half],
            device_id=chip(0, dz, dy, c),
            device_id_type=MESH,
        )

    def first_copy(n, half):
        dz, dy = AROUND[n]
        return pltpu.make_async_remote_copy(
            src_ref=kv.at[half],
            dst_ref=kv.at[2 * (1 + n) + half],
            send_sem=kv_send.at[2 * n + half],
            recv_sem=kv_recv.at[2 * (1 + n) + half],
            device_id=chip(0, dz, dy, c),
            device_id_type=MESH,
        )

    def arrival(slot):
        return pltpu.make_async_remote_copy(
            src_ref=kv.at[slot],
            dst_ref=kv.at[slot],
            send_sem=kv_send.at[0],
            recv_sem=kv_recv.at[slot],
            device_id=chip(0, 0, 0, sib),
            device_id_type=MESH,
        )

    to_sib = pltpu.make_async_remote_copy(
        src_ref=other, dst_ref=kv.at[c], send_sem=sib_send, recv_sem=kv_recv.at[c],
        device_id=chip(0, 0, 0, sib), device_id_type=MESH,
    )
    to_sib.start()
    q_out = pltpu.make_async_remote_copy(
        src_ref=q_hbm.at[:, pl.ds(pl.multiple_of(sib * wide, wide), wide)],
        dst_ref=qraw.at[c],
        send_sem=q_send,
        recv_sem=q_recv,
        device_id=chip(0, 0, 0, sib),
        device_id_type=MESH,
    )
    q_out.start()
    for n in range(4):
        first_copy(n, c).start()
    arrival(sib).wait_recv()
    for n in range(4):
        first_copy(n, sib).start()

    lane = lax.broadcasted_iota(jnp.int32, (16, HD), 1)
    own = jnp.zeros((16, HD), jnp.float32)
    for run in range(4):
        at = 2 * ROWS + 16 * (run % 2)
        own = jnp.where(lane == run, kv[run // 2, at : at + 16, :].astype(jnp.float32), own)

    def fill_bias(slot):
        for run in range(2):
            block = kv[slot, 2 * ROWS + 16 * run : 2 * ROWS + 16 * run + 16, :].astype(jnp.float32)
            tile = jnp.where(block < own, 0.0, HIDDEN).astype(jnp.bfloat16)
            for r in range(8):
                bias[slot, run * HD + 16 * r : run * HD + 16 * r + 16, :] = tile

    q_mine.wait()
    q_in = pltpu.make_async_remote_copy(
        src_ref=qraw.at[sib], dst_ref=qraw.at[sib], send_sem=q_send, recv_sem=q_recv,
        device_id=chip(0, 0, 0, sib), device_id_type=MESH,
    )
    q_in.wait_recv()
    scale = 1.4426950408889634 / HD**0.5
    lanes = lax.broadcasted_iota(jnp.int32, (TILE, HD), 1)
    row = lax.rem(lax.broadcasted_iota(jnp.int32, (TILE, HD), 0), PART)

    def begin(tile, carry):
        shard, part = tile // 8, lax.rem(tile, 8)
        run = part // 4
        rows = pl.ds(pl.multiple_of(part * PART, PART), PART)
        for h in range(GROUP):
            piece = qraw[shard, rows, h * HD : (h + 1) * HD].astype(jnp.float32) * scale
            qx[tile, h * PART : (h + 1) * PART, :HD] = piece.astype(jnp.bfloat16)
        qx[tile, :, HD:] = jnp.where(lanes == 2 * shard + run, 1.0, 0.0).astype(jnp.bfloat16)
        keys = pl.ds(pl.multiple_of(run * HD, HD), HD)
        vals = pl.ds(pl.multiple_of(ROWS + run * HD, HD), HD)
        diag = dot_nt(qx[tile, :, :HD], kv[shard, keys, :])
        diag = jnp.where(lanes <= row + lax.rem(part, 4) * PART, diag, HIDDEN)
        k, v = pair([0, 1])
        s = jnp.concatenate([diag, dot_nt(qx[tile], k)], axis=1)
        high = jnp.broadcast_to(jnp.max(s, axis=1, keepdims=True), (TILE, HD))
        p = jnp.exp2(s - high[:, :1]).astype(jnp.bfloat16)
        v = jnp.concatenate([kv[shard, vals, :], v], axis=0)
        top[tile] = high
        acc[tile] = dot(p, jnp.concatenate([v, jnp.ones_like(v)], axis=1))
        return carry

    def slots_of(places):
        return [2 * place + half for place in places for half in range(2)]

    def pair(slots):
        k = jnp.concatenate([kv[slot, :ROWS, :] for slot in slots], axis=0)
        b = jnp.concatenate([bias[slot] for slot in slots], axis=0)
        v = jnp.concatenate([kv[slot, ROWS : 2 * ROWS, :] for slot in slots], axis=0)
        return jnp.concatenate([k, b], axis=1), v

    for slot in range(2):
        fill_bias(slot)
    lax.fori_loop(0, TILES, begin, 0, unroll=4)

    scores, weights, fades = (s_even, s_odd), (p_even, p_odd), (f_even, f_odd)

    def score(tile, slots, b):
        k, _ = pair(slots)
        scores[b][:, : ROWS * len(slots)] = dot_nt(qx[tile], k)

    def weigh(tile, count, b):
        s = scores[b][:, : ROWS * count]
        before = top[tile]
        high = jnp.maximum(before, jnp.max(s, axis=1, keepdims=True))
        weights[b][:, : ROWS * count] = jnp.exp2(s - high[:, :1]).astype(jnp.bfloat16)
        fades[b][...] = jnp.exp2(before - high)
        top[tile] = high

    def gather(tile, slots, b):
        _, v = pair(slots)
        fade = fades[b][...]
        acc[tile] = acc[tile] * jnp.concatenate([fade, fade], axis=1) + dot(
            weights[b][:, : ROWS * len(slots)], jnp.concatenate([v, jnp.ones_like(v)], axis=1)
        )

    def serve(places, halves=(0, 1)):
        for place in places:
            for half in halves:
                arrival(2 * place + half).wait_recv()
                for index, send in enumerate(SENDS):
                    if send[:2] == (place, half):
                        kv_copy(index).start()
                fill_bias(2 * place + half)

    def slots_at(turn):
        step = turn // 2
        half = jnp.where(lax.rem(step, 2) == 0, c, sib)
        start = jnp.where(step < 4, 2 + 8 * (step // 2) + half, 4 * step + 2)
        stride = jnp.where(step < 4, 2, 1)
        return [start + stride * a for a in range(4)]

    def tile_at(turn, u):
        return lax.rem(turn, 2) * BAND + u

    for core in range(2):

        @pl.when(c == core)
        def _():
            serve((1, 2, 3, 4), (core,))

    score(0, slots_at(0), 0)

    def early(turn, carry):
        for i, places, which in SERVED:
            if which == 2:

                @pl.when(turn == i)
                def _():
                    serve(places)

            else:
                for core in range(2):

                    @pl.when((turn == i) & (c == core))
                    def _():
                        serve(places, ((core + which) % 2,))

        here = slots_at(turn)
        before = slots_at(jnp.maximum(turn - 1, 0))
        after = slots_at(jnp.minimum(turn + 1, 2 * STEPS - 1))
        for u in range(BAND):
            now, other_one = u % 2, (u + 1) % 2
            if u + 1 < BAND:
                score(tile_at(turn, u + 1), here, other_one)
            else:
                score(tile_at(turn + 1, 0), after, other_one)
            if u:
                gather(tile_at(turn, u - 1), here, other_one)
            else:
                gather(tile_at(turn + 1, BAND - 1), before, other_one)
            weigh(tile_at(turn, u), 4, now)
        return carry

    weights[1][...] = jnp.zeros_like(weights[1])
    fades[1][...] = jnp.ones_like(fades[1])
    lax.fori_loop(0, 2 * STEPS, early, 0)
    gather(TILES - 1, slots_at(2 * STEPS - 1), 1)
    serve((15,))

    def landing(half, source):
        cols = pl.ds(pl.multiple_of(source * wide, wide), wide)
        return att.at[pl.ds(pl.multiple_of(half * PART, PART), PART), cols]

    def own_copy(half):
        return pltpu.make_async_copy(
            obuf.at[c * 8 + x * 2 + half], landing(half, 2 * x + c), out_sem.at[half]
        )

    def att_copy(g, dx):
        half, shard = g // 2, lax.rem(c + 1 + g, 2)
        there = lax.rem(x + dx, 4)
        tile = shard * 8 + there * 2 + half
        return tile, pltpu.make_async_remote_copy(
            src_ref=obuf.at[tile],
            dst_ref=landing(half, 2 * x + c),
            send_sem=att_send.at[tile],
            recv_sem=att_recv.at[half, 2 * x + c],
            device_id=chip(dx, 0, 0, shard),
            device_id_type=MESH,
        )

    def finish(g, carry):
        half, shard = g // 2, lax.rem(c + 1 + g, 2)
        last = slots_of(LAST)
        tiles = [shard * 8 + quarter * 2 + half for quarter in range(4)]
        later = jnp.minimum(g + 1, 3)
        following = lax.rem(c + 1 + later, 2) * 8 + later // 2
        for u in range(4):
            score(tiles[u + 1] if u < 3 else following, last, (u + 1) % 2)
            if u:
                gather(tiles[u - 1], last, (u + 1) % 2)
            weigh(tiles[u], len(last), u % 2)
        gather(tiles[3], last, 1)
        for tile in tiles:
            both = acc[tile]
            o = (both[:, :HD] / both[:, HD:]).astype(jnp.bfloat16)
            for h in range(GROUP):
                obuf[tile, :, h * HD : (h + 1) * HD] = o[h * PART : (h + 1) * PART, :]
        for dx in (1, 2, 3):
            att_copy(g, dx)[1].start()

        @pl.when(lax.rem(g, 2) == 0)
        def _():
            att_copy(g, 0)[1].start()

        @pl.when(lax.rem(g, 2) == 1)
        def _():
            own_copy(half).start()

        return carry

    score(lax.rem(c + 1, 2) * 8, slots_of(LAST), 0)
    lax.fori_loop(0, 4, finish, 0)

    for half in range(2):
        for n in range(1, 8):
            source = lax.rem(2 * x + c + n, 8)
            pltpu.make_async_remote_copy(
                src_ref=landing(half, source), dst_ref=landing(half, source), send_sem=q_send,
                recv_sem=att_recv.at[half, source], device_id=chip(0, 0, 0, sib), device_id_type=MESH,
            ).wait_recv()
    to_sib.wait_send()
    q_out.wait_send()
    for n in range(4):
        for half in range(2):
            first_copy(n, half).wait_send()
    for index in range(len(FIRST), len(SENDS)):
        kv_copy(index).wait_send()

    def sent(g, carry):
        for dx in (1, 2, 3):
            att_copy(g, dx)[1].wait_send()

        @pl.when(lax.rem(g, 2) == 0)
        def _():
            att_copy(g, 0)[1].wait_send()

        return carry

    lax.fori_loop(0, 4, sent, 0)
    for half in range(2):
        own_copy(half).wait()


def update(att_ref, res_ref, gain_ref, stream_ref, normed_ref):
    stream = res_ref[...] + att_ref[...].astype(jnp.float32)
    stream_ref[...] = stream
    inv = lax.rsqrt(jnp.mean(stream * stream, axis=1, keepdims=True) + 1e-05)
    normed_ref[...] = (stream * inv * gain_ref[...]).astype(jnp.bfloat16)


def per_device(queries, keys, values, positions, residual, gain):
    width = residual.shape[2]
    rows = residual.shape[1]
    hbm = pl.BlockSpec(memory_space=pl.ANY)
    vmem = pl.BlockSpec(memory_space=pltpu.VMEM)
    dma = pltpu.SemaphoreType.DMA
    bf16, f32 = jnp.bfloat16, jnp.float32
    attended = pl.pallas_call(
        kernel,
        out_shape=jax.ShapeDtypeStruct((rows, width), bf16),
        in_specs=[vmem, hbm, hbm, hbm],
        out_specs=hbm,
        scratch_shapes=[
            pltpu.VMEM((32, MSG, HD), bf16),
            pltpu.VMEM((MSG, HD), bf16),
            pltpu.VMEM((32, ROWS, HD), bf16),
            pltpu.VMEM((2, ROWS, GROUP * HD), bf16),
            pltpu.VMEM((TILES, TILE, 2 * HD), bf16),
            pltpu.VMEM((TILES, TILE, HD), f32),
            pltpu.VMEM((TILES, TILE, 2 * HD), f32),
            pltpu.VMEM((TILES, PART, GROUP * HD), bf16),
            pltpu.VMEM((TILE, 6 * ROWS), f32),
            pltpu.VMEM((TILE, 6 * ROWS), f32),
            pltpu.VMEM((TILE, 6 * ROWS), bf16),
            pltpu.VMEM((TILE, 6 * ROWS), bf16),
            pltpu.VMEM((TILE, HD), f32),
            pltpu.VMEM((TILE, HD), f32),
            dma((5,)),
            dma((len(SENDS),)),
            dma((32,)),
            dma,
            dma,
            dma,
            dma((TILES,)),
            dma((2, 8)),
            dma((2,)),
        ],
        compiler_params=pltpu.CompilerParams(
            collective_id=0, has_side_effects=True, vmem_limit_bytes=60 * 2**20
        ),
    )(positions.reshape(2, HD), queries, keys, values)
    block = 16
    band = pl.BlockSpec((block, width), lambda i: (i, 0))
    stream, normed = pl.pallas_call(
        update,
        grid=(rows // block,),
        out_shape=(
            jax.ShapeDtypeStruct((rows, width), f32),
            jax.ShapeDtypeStruct((rows, width), bf16),
        ),
        in_specs=[band, band, pl.BlockSpec((1, width), lambda i: (0, 0))],
        out_specs=(band, band),
    )(attended, residual[0], gain.reshape(1, width))
    return (stream[None], normed[None])


def solution(mesh):
    both = ("outer", "inner")
    return jax.shard_map(
        per_device,
        mesh=mesh,
        in_specs=(P(both, "head"), P(both, "head"), P(both, "head"), P(both), P(both, "head", None), P()),
        out_specs=(P(both, "head", None), P(both, "head", None)),
        check_vma=False,
    )
```

```python
import jax
import jax.numpy as jnp
from jax import lax
from jax.experimental import pallas as pl
from jax.experimental.pallas import tpu as pltpu
from jax.sharding import PartitionSpec as P

HD = 128
ROWS = 256
GROUP = 8
PART = 32
TILES = 16
TILE = GROUP * PART
MSG = 2 * ROWS + 32
STEPS = 5
HIDDEN = -1e30
MESH = pl.DeviceIdType.MESH

PLACES = [(0, 0), (1, 0), (3, 0), (0, 1), (0, 3), (2, 0), (0, 2),
          (1, 1), (1, 3), (3, 1), (3, 3), (2, 1), (2, 3), (1, 2), (3, 2), (2, 2)]

SERVED = [(1, (1, 2, 3, 4), 1), (3, (5, 6, 7, 8), 0), (4, (9, 10), 0), (5, (5, 6, 7, 8), 1), (6, (9, 10), 1),
          (8, (11, 14), 2), (9, (12, 13), 2)]
LATER = (9, 10)
LAST = (11, 12, 13, 14, 15)
BAND = TILES // 2


def dot(a, b):
    return jnp.dot(a, b, preferred_element_type=jnp.float32)


def dot_nt(a, b):
    return lax.dot_general(a, b, (((1,), (1,)), ((), ())), preferred_element_type=jnp.float32)


def forwards(place):
    out = []
    here = PLACES[place]
    for half in range(2):
        a, b = here if half == 0 else here[::-1]
        there = []
        if a == 0 and b == 0:
            there += [(1, 0), (3, 0)]
        if a == (1, 3)[half] and b == 0:
            there.append((2, 0))
        if b == 0:
            there += [(a, 1), (a, 3)]
        if b == (1 if a in ((0, 2, 3), (3,))[half] else 3):
            there.append((a, 2))
        for na, nb in there:
            da, db = (na - a) % 4, (nb - b) % 4
            step, new = ((da, db), (na, nb)) if half == 0 else ((db, da), (nb, na))
            out.append((half,) + step + (PLACES.index(new),))
    return out


FIRST = forwards(0)
SENDS = [(j,) + f for j in range(16) for f in forwards(j)]
AROUND = [(1, 0), (3, 0), (0, 1), (0, 3)]


def kernel(
    pos_ref, q_hbm, k_hbm, v_hbm, att,
    kv, other, bias, qraw, qx, top, acc, obuf, s_even, s_odd, p_even, p_odd, f_even, f_odd,
    stage_sem, kv_send, kv_recv, q_send, q_recv, sib_send, att_send, att_recv, out_sem,
):
    x = lax.axis_index("head")
    outer = lax.axis_index("outer")
    inner = lax.axis_index("inner")
    y_hi, z = outer // 4, lax.rem(outer, 4)
    y_lo, c = inner // 2, lax.rem(inner, 2)
    y = y_hi * 2 + y_lo
    sib = 1 - c

    def chip(dx, dz, dy, core):
        zz, yy = lax.rem(z + dz, 4), lax.rem(y + dy, 4)
        return (lax.rem(x + dx, 4), (yy // 2) * 4 + zz, lax.rem(yy, 2) * 2 + core)

    mine = pl.ds(pl.multiple_of(c * HD, HD), HD)
    theirs = pl.ds(pl.multiple_of(sib * HD, HD), HD)
    stage = [
        pltpu.make_async_copy(k_hbm.at[:, mine], kv.at[c, pl.ds(0, ROWS)], stage_sem.at[0]),
        pltpu.make_async_copy(v_hbm.at[:, mine], kv.at[c, pl.ds(ROWS, ROWS)], stage_sem.at[1]),
        pltpu.make_async_copy(k_hbm.at[:, theirs], other.at[pl.ds(0, ROWS)], stage_sem.at[2]),
        pltpu.make_async_copy(v_hbm.at[:, theirs], other.at[pl.ds(ROWS, ROWS)], stage_sem.at[3]),
    ]
    for copy in stage:
        copy.start()
    wide = GROUP * HD
    q_mine = pltpu.make_async_copy(
        q_hbm.at[:, pl.ds(pl.multiple_of(c * wide, wide), wide)], qraw.at[c], stage_sem.at[4]
    )
    q_mine.start()

    partners = [chip(0, 0, 0, sib)]
    partners += [chip(0, dz, dy, c) for dz, dy in AROUND]
    partners += [chip(dx, 0, 0, core) for dx in (1, 2, 3) for core in (c, sib)]
    barrier = pltpu.get_barrier_semaphore()
    for partner in partners:
        pl.semaphore_signal(barrier, inc=1, device_id=partner, device_id_type=MESH)

    for run in range(2):
        block = (pos_ref[run : run + 1, :] >> 7).astype(jnp.float32)
        tile = jnp.broadcast_to(block, (16, HD)).astype(jnp.bfloat16)
        kv[c, 2 * ROWS + 16 * run : 2 * ROWS + 16 * run + 16, :] = tile
        other[2 * ROWS + 16 * run : 2 * ROWS + 16 * run + 16, :] = tile
    for copy in stage:
        copy.wait()
    pl.semaphore_wait(barrier, len(partners))

    def kv_copy(index):
        place, half, dz, dy, there = SENDS[index]
        return pltpu.make_async_remote_copy(
            src_ref=kv.at[2 * place + half],
            dst_ref=kv.at[2 * there + half],
            send_sem=kv_send.at[index],
            recv_sem=kv_recv.at[2 * there + half],
            device_id=chip(0, dz, dy, c),
            device_id_type=MESH,
        )

    def first_copy(n, half):
        dz, dy = AROUND[n]
        return pltpu.make_async_remote_copy(
            src_ref=kv.at[half],
            dst_ref=kv.at[2 * (1 + n) + half],
            send_sem=kv_send.at[2 * n + half],
            recv_sem=kv_recv.at[2 * (1 + n) + half],
            device_id=chip(0, dz, dy, c),
            device_id_type=MESH,
        )

    def arrival(slot):
        return pltpu.make_async_remote_copy(
            src_ref=kv.at[slot],
            dst_ref=kv.at[slot],
            send_sem=kv_send.at[0],
            recv_sem=kv_recv.at[slot],
            device_id=chip(0, 0, 0, sib),
            device_id_type=MESH,
        )

    to_sib = pltpu.make_async_remote_copy(
        src_ref=other, dst_ref=kv.at[c], send_sem=sib_send, recv_sem=kv_recv.at[c],
        device_id=chip(0, 0, 0, sib), device_id_type=MESH,
    )
    to_sib.start()
    q_out = pltpu.make_async_remote_copy(
        src_ref=q_hbm.at[:, pl.ds(pl.multiple_of(sib * wide, wide), wide)],
        dst_ref=qraw.at[c],
        send_sem=q_send,
        recv_sem=q_recv,
        device_id=chip(0, 0, 0, sib),
        device_id_type=MESH,
    )
    q_out.start()
    for n in range(4):
        first_copy(n, c).start()
    arrival(sib).wait_recv()
    for n in range(4):
        first_copy(n, sib).start()

    lane = lax.broadcasted_iota(jnp.int32, (16, HD), 1)
    own = jnp.zeros((16, HD), jnp.float32)
    for run in range(4):
        at = 2 * ROWS + 16 * (run % 2)
        own = jnp.where(lane == run, kv[run // 2, at : at + 16, :].astype(jnp.float32), own)

    def fill_bias(slot):
        for run in range(2):
            block = kv[slot, 2 * ROWS + 16 * run : 2 * ROWS + 16 * run + 16, :].astype(jnp.float32)
            tile = jnp.where(block < own, 0.0, HIDDEN).astype(jnp.bfloat16)
            for r in range(8):
                bias[slot, run * HD + 16 * r : run * HD + 16 * r + 16, :] = tile

    q_mine.wait()
    q_in = pltpu.make_async_remote_copy(
        src_ref=qraw.at[sib], dst_ref=qraw.at[sib], send_sem=q_send, recv_sem=q_recv,
        device_id=chip(0, 0, 0, sib), device_id_type=MESH,
    )
    q_in.wait_recv()
    scale = 1.4426950408889634 / HD**0.5
    lanes = lax.broadcasted_iota(jnp.int32, (TILE, HD), 1)
    row = lax.rem(lax.broadcasted_iota(jnp.int32, (TILE, HD), 0), PART)

    def begin(tile, carry):
        shard, part = tile // 8, lax.rem(tile, 8)
        rows = pl.ds(pl.multiple_of(part * PART, PART), PART)
        for h in range(GROUP):
            piece = qraw[shard, rows, h * HD : (h + 1) * HD].astype(jnp.float32) * scale
            qx[tile, h * PART : (h + 1) * PART, :HD] = piece.astype(jnp.bfloat16)
        qx[tile, :, HD:] = jnp.where(lanes == 2 * shard + part // 4, 1.0, 0.0).astype(jnp.bfloat16)
        top[tile] = jnp.full((TILE, HD), HIDDEN, jnp.float32)
        acc[tile] = jnp.zeros((TILE, 2 * HD), jnp.float32)
        return carry

    def slots_of(places):
        return [2 * place + half for place in places for half in range(2)]

    def pair(slots):
        k = jnp.concatenate([kv[slot, :ROWS, :] for slot in slots], axis=0)
        b = jnp.concatenate([bias[slot] for slot in slots], axis=0)
        v = jnp.concatenate([kv[slot, ROWS : 2 * ROWS, :] for slot in slots], axis=0)
        return jnp.concatenate([k, b], axis=1), v

    for slot in range(2):
        fill_bias(slot)
    lax.fori_loop(0, TILES, begin, 0, unroll=2)

    scores, weights, fades = (s_even, s_odd), (p_even, p_odd), (f_even, f_odd)

    def score(tile, slots, b):
        k, _ = pair(slots)
        scores[b][:, : ROWS * len(slots)] = dot_nt(qx[tile], k)

    def weigh(tile, keys, b):
        s = scores[b][:, :keys]
        before = top[tile]
        high = jnp.maximum(before, jnp.max(s, axis=1, keepdims=True))
        weights[b][:, :keys] = jnp.exp2(s - high[:, :1]).astype(jnp.bfloat16)
        fades[b][...] = jnp.exp2(before - high)
        top[tile] = high

    def add(tile, v, b):
        fade = fades[b][...]
        acc[tile] = acc[tile] * jnp.concatenate([fade, fade], axis=1) + dot(
            weights[b][:, : v.shape[0]], jnp.concatenate([v, jnp.ones_like(v)], axis=1)
        )

    def gather(tile, slots, b):
        add(tile, pair(slots)[1], b)

    def score_own(tile, b):
        shard, part = tile // 8, lax.rem(tile, 8)
        keys = pl.ds(pl.multiple_of(part // 4 * HD, HD), HD)
        diag = dot_nt(qx[tile, :, :HD], kv[shard, keys, :])
        scores[b][:, :HD] = jnp.where(lanes <= row + lax.rem(part, 4) * PART, diag, HIDDEN)
        scores[b][:, HD : HD + 2 * ROWS] = dot_nt(qx[tile], pair([0, 1])[0])

    def gather_own(tile, b):
        vals = pl.ds(pl.multiple_of(ROWS + lax.rem(tile, 8) // 4 * HD, HD), HD)
        add(tile, jnp.concatenate([kv[tile // 8, vals, :], pair([0, 1])[1]], axis=0), b)

    def nothing_before():
        weights[1][...] = jnp.zeros_like(weights[1])
        fades[1][...] = jnp.ones_like(fades[1])

    def own_turn(turn, carry):
        for u in range(BAND):
            tile = turn * BAND + u
            score_own(jnp.minimum(tile + 1, TILES - 1), (u + 1) % 2)
            gather_own(jnp.maximum(tile - 1, 0), (u + 1) % 2)
            weigh(tile, HD + 2 * ROWS, u % 2)
        return carry

    nothing_before()
    score_own(0, 0)
    lax.fori_loop(0, 2, own_turn, 0)
    gather_own(TILES - 1, 1)

    def serve(places, halves=(0, 1)):
        for place in places:
            for half in halves:
                arrival(2 * place + half).wait_recv()
                for index, send in enumerate(SENDS):
                    if send[:2] == (place, half) and (place > 4 or send[4] not in LATER):
                        kv_copy(index).start()
                fill_bias(2 * place + half)

    def send_later(half):
        for index, send in enumerate(SENDS):
            if 0 < send[0] < 5 and send[1] == half and send[4] in LATER:
                kv_copy(index).start()

    def slots_at(turn):
        step = turn // 2
        half = jnp.where(lax.rem(step, 2) == 0, c, sib)
        start = jnp.where(step < 4, 2 + 8 * (step // 2) + half, 4 * step + 2)
        stride = jnp.where(step < 4, 2, 1)
        return [start + stride * a for a in range(4)]

    def tile_at(turn, u):
        return lax.rem(turn, 2) * BAND + u

    for core in range(2):

        @pl.when(c == core)
        def _():
            serve((1, 2, 3, 4), (core,))

    score(0, slots_at(0), 0)

    def early(turn, carry):
        for i, places, which in SERVED:
            if which == 2:

                @pl.when(turn == i)
                def _():
                    serve(places)

            else:
                for core in range(2):

                    @pl.when((turn == i) & (c == core))
                    def _():
                        serve(places, ((core + which) % 2,))

        for core in range(2):
            for i in (1, 2):

                @pl.when((turn == i) & (c == core))
                def _():
                    send_later((core + i + 1) % 2)

        here = slots_at(turn)
        before = slots_at(jnp.maximum(turn - 1, 0))
        after = slots_at(jnp.minimum(turn + 1, 2 * STEPS - 1))
        for u in range(BAND):
            now, other_one = u % 2, (u + 1) % 2
            if u + 1 < BAND:
                score(tile_at(turn, u + 1), here, other_one)
            else:
                score(tile_at(turn + 1, 0), after, other_one)
            if u:
                gather(tile_at(turn, u - 1), here, other_one)
            else:
                gather(tile_at(turn + 1, BAND - 1), before, other_one)
            weigh(tile_at(turn, u), 4 * ROWS, now)
        return carry

    nothing_before()
    lax.fori_loop(0, 2 * STEPS, early, 0)
    gather(TILES - 1, slots_at(2 * STEPS - 1), 1)
    serve((15,))

    def landing(half, source):
        cols = pl.ds(pl.multiple_of(source * wide, wide), wide)
        return att.at[pl.ds(pl.multiple_of(half * PART, PART), PART), cols]

    def own_copy(half):
        return pltpu.make_async_copy(
            obuf.at[c * 8 + x * 2 + half], landing(half, 2 * x + c), out_sem.at[half]
        )

    def att_copy(g, dx):
        half, shard = g // 2, lax.rem(c + 1 + g, 2)
        there = lax.rem(x + dx, 4)
        tile = shard * 8 + there * 2 + half
        return tile, pltpu.make_async_remote_copy(
            src_ref=obuf.at[tile],
            dst_ref=landing(half, 2 * x + c),
            send_sem=att_send.at[tile],
            recv_sem=att_recv.at[half, 2 * x + c],
            device_id=chip(dx, 0, 0, shard),
            device_id_type=MESH,
        )

    def finish(g, carry):
        half, shard = g // 2, lax.rem(c + 1 + g, 2)
        last = slots_of(LAST)
        tiles = [shard * 8 + quarter * 2 + half for quarter in range(4)]
        later = jnp.minimum(g + 1, 3)
        following = lax.rem(c + 1 + later, 2) * 8 + later // 2
        for u in range(4):
            score(tiles[u + 1] if u < 3 else following, last, (u + 1) % 2)
            if u:
                gather(tiles[u - 1], last, (u + 1) % 2)
            weigh(tiles[u], len(last) * ROWS, u % 2)
        gather(tiles[3], last, 1)
        for tile in tiles:
            both = acc[tile]
            o = (both[:, :HD] / both[:, HD:]).astype(jnp.bfloat16)
            for h in range(GROUP):
                obuf[tile, :, h * HD : (h + 1) * HD] = o[h * PART : (h + 1) * PART, :]
        for dx in (2, 1, 3):
            att_copy(g, dx)[1].start()

        @pl.when(lax.rem(g, 2) == 0)
        def _():
            att_copy(g, 0)[1].start()

        @pl.when(lax.rem(g, 2) == 1)
        def _():
            own_copy(half).start()

        return carry

    score(lax.rem(c + 1, 2) * 8, slots_of(LAST), 0)
    lax.fori_loop(0, 4, finish, 0)

    for half in range(2):
        for n in range(1, 8):
            source = lax.rem(2 * x + c + n, 8)
            pltpu.make_async_remote_copy(
                src_ref=landing(half, source), dst_ref=landing(half, source), send_sem=q_send,
                recv_sem=att_recv.at[half, source], device_id=chip(0, 0, 0, sib), device_id_type=MESH,
            ).wait_recv()
    to_sib.wait_send()
    q_out.wait_send()
    for n in range(4):
        for half in range(2):
            first_copy(n, half).wait_send()
    for index in range(len(FIRST), len(SENDS)):
        kv_copy(index).wait_send()

    def sent(g, carry):
        for dx in (1, 2, 3):
            att_copy(g, dx)[1].wait_send()

        @pl.when(lax.rem(g, 2) == 0)
        def _():
            att_copy(g, 0)[1].wait_send()

        return carry

    lax.fori_loop(0, 4, sent, 0)
    for half in range(2):
        own_copy(half).wait()


def per_device(queries, keys, values, positions, residual, gain):
    width = residual.shape[2]
    rows = residual.shape[1]
    hbm = pl.BlockSpec(memory_space=pl.ANY)
    vmem = pl.BlockSpec(memory_space=pltpu.VMEM)
    dma = pltpu.SemaphoreType.DMA
    bf16, f32 = jnp.bfloat16, jnp.float32
    attended = pl.pallas_call(
        kernel,
        out_shape=jax.ShapeDtypeStruct((rows, width), bf16),
        in_specs=[vmem, hbm, hbm, hbm],
        out_specs=hbm,
        scratch_shapes=[
            pltpu.VMEM((32, MSG, HD), bf16),
            pltpu.VMEM((MSG, HD), bf16),
            pltpu.VMEM((32, ROWS, HD), bf16),
            pltpu.VMEM((2, ROWS, GROUP * HD), bf16),
            pltpu.VMEM((TILES, TILE, 2 * HD), bf16),
            pltpu.VMEM((TILES, TILE, HD), f32),
            pltpu.VMEM((TILES, TILE, 2 * HD), f32),
            pltpu.VMEM((TILES, PART, GROUP * HD), bf16),
            pltpu.VMEM((TILE, 10 * ROWS), f32),
            pltpu.VMEM((TILE, 10 * ROWS), f32),
            pltpu.VMEM((TILE, 10 * ROWS), bf16),
            pltpu.VMEM((TILE, 10 * ROWS), bf16),
            pltpu.VMEM((TILE, HD), f32),
            pltpu.VMEM((TILE, HD), f32),
            dma((5,)),
            dma((len(SENDS),)),
            dma((32,)),
            dma,
            dma,
            dma,
            dma((TILES,)),
            dma((2, 8)),
            dma((2,)),
        ],
        compiler_params=pltpu.CompilerParams(
            collective_id=0, has_side_effects=True, vmem_limit_bytes=60 * 2**20
        ),
    )(positions.reshape(2, HD), queries, keys, values)
    stream = residual[0] + attended.astype(f32)
    inv = lax.rsqrt(jnp.mean(stream * stream, axis=1, keepdims=True) + 1e-05)
    normed = (stream * inv * gain).astype(bf16)
    return (stream[None], normed[None])


def solution(mesh):
    both = ("outer", "inner")
    return jax.shard_map(
        per_device,
        mesh=mesh,
        in_specs=(P(both, "head"), P(both, "head"), P(both, "head"), P(both), P(both, "head", None), P()),
        out_specs=(P(both, "head", None), P(both, "head", None)),
        check_vma=False,
    )
```

```python
import jax
import jax.numpy as jnp
from jax import lax
from jax.experimental import pallas as pl
from jax.experimental.pallas import tpu as pltpu
from jax.sharding import PartitionSpec as P

HD = 128
ROWS = 256
GROUP = 8
PART = 32
TILES = 16
TILE = GROUP * PART
MSG = 2 * ROWS + 32
STEPS = 5
HIDDEN = -1e30
MESH = pl.DeviceIdType.MESH

PLACES = [(0, 0), (1, 0), (3, 0), (0, 1), (0, 3), (2, 0), (0, 2),
          (1, 1), (1, 3), (3, 1), (3, 3), (2, 1), (2, 3), (1, 2), (3, 2), (2, 2)]

SERVED = [(1, (1, 2, 3, 4), 1), (3, (5, 6, 7, 8), 0), (4, (9, 10), 0), (5, (5, 6, 7, 8), 1), (6, (9, 10), 1),
          (8, (11, 14), 2), (9, (12, 13), 2)]
LATER = (9, 10)
LAST = (11, 12, 13, 14, 15)
BAND = TILES // 2


def dot(a, b):
    return jnp.dot(a, b, preferred_element_type=jnp.float32)


def dot_nt(a, b):
    return lax.dot_general(a, b, (((1,), (1,)), ((), ())), preferred_element_type=jnp.float32)


def forwards(place):
    out = []
    here = PLACES[place]
    for half in range(2):
        a, b = here if half == 0 else here[::-1]
        there = []
        if a == 0 and b == 0:
            there += [(1, 0), (3, 0)]
        if a == (1, 3)[half] and b == 0:
            there.append((2, 0))
        if b == 0:
            there += [(a, 1), (a, 3)]
        if b == (1 if a in ((0, 2, 3), (3,))[half] else 3):
            there.append((a, 2))
        for na, nb in there:
            da, db = (na - a) % 4, (nb - b) % 4
            step, new = ((da, db), (na, nb)) if half == 0 else ((db, da), (nb, na))
            out.append((half,) + step + (PLACES.index(new),))
    return out


FIRST = forwards(0)
SENDS = [(j,) + f for j in range(16) for f in forwards(j)]
AROUND = [(1, 0), (3, 0), (0, 1), (0, 3)]


def kernel(
    pos_ref, q_hbm, k_hbm, v_hbm, att,
    kv, other, bias, qraw, qx, top, acc, obuf, s_even, s_odd, p_even, p_odd, f_even, f_odd,
    stage_sem, kv_send, kv_recv, q_send, q_recv, sib_send, att_send, att_recv, out_sem,
):
    x = lax.axis_index("head")
    outer = lax.axis_index("outer")
    inner = lax.axis_index("inner")
    y_hi, z = outer // 4, lax.rem(outer, 4)
    y_lo, c = inner // 2, lax.rem(inner, 2)
    y = y_hi * 2 + y_lo
    sib = 1 - c

    def chip(dx, dz, dy, core):
        zz, yy = lax.rem(z + dz, 4), lax.rem(y + dy, 4)
        return (lax.rem(x + dx, 4), (yy // 2) * 4 + zz, lax.rem(yy, 2) * 2 + core)

    mine = pl.ds(pl.multiple_of(c * HD, HD), HD)
    theirs = pl.ds(pl.multiple_of(sib * HD, HD), HD)
    stage = [
        pltpu.make_async_copy(k_hbm.at[:, mine], kv.at[c, pl.ds(0, ROWS)], stage_sem.at[0]),
        pltpu.make_async_copy(v_hbm.at[:, mine], kv.at[c, pl.ds(ROWS, ROWS)], stage_sem.at[1]),
        pltpu.make_async_copy(k_hbm.at[:, theirs], other.at[pl.ds(0, ROWS)], stage_sem.at[2]),
        pltpu.make_async_copy(v_hbm.at[:, theirs], other.at[pl.ds(ROWS, ROWS)], stage_sem.at[3]),
    ]
    for copy in stage:
        copy.start()
    wide = GROUP * HD
    q_mine = pltpu.make_async_copy(
        q_hbm.at[:, pl.ds(pl.multiple_of(c * wide, wide), wide)], qraw.at[c], stage_sem.at[4]
    )
    q_mine.start()

    partners = [chip(0, 0, 0, sib)]
    partners += [chip(0, dz, dy, c) for dz, dy in AROUND]
    partners += [chip(dx, 0, 0, core) for dx in (1, 2, 3) for core in (c, sib)]
    barrier = pltpu.get_barrier_semaphore()
    for partner in partners:
        pl.semaphore_signal(barrier, inc=1, device_id=partner, device_id_type=MESH)

    for run in range(2):
        block = (pos_ref[run : run + 1, :] >> 7).astype(jnp.float32)
        tile = jnp.broadcast_to(block, (16, HD)).astype(jnp.bfloat16)
        kv[c, 2 * ROWS + 16 * run : 2 * ROWS + 16 * run + 16, :] = tile
        other[2 * ROWS + 16 * run : 2 * ROWS + 16 * run + 16, :] = tile
    for copy in stage:
        copy.wait()
    pl.semaphore_wait(barrier, len(partners))

    def kv_copy(index):
        place, half, dz, dy, there = SENDS[index]
        return pltpu.make_async_remote_copy(
            src_ref=kv.at[2 * place + half],
            dst_ref=kv.at[2 * there + half],
            send_sem=kv_send.at[index],
            recv_sem=kv_recv.at[2 * there + half],
            device_id=chip(0, dz, dy, c),
            device_id_type=MESH,
        )

    def first_copy(n, half):
        dz, dy = AROUND[n]
        return pltpu.make_async_remote_copy(
            src_ref=kv.at[half],
            dst_ref=kv.at[2 * (1 + n) + half],
            send_sem=kv_send.at[2 * n + half],
            recv_sem=kv_recv.at[2 * (1 + n) + half],
            device_id=chip(0, dz, dy, c),
            device_id_type=MESH,
        )

    def arrival(slot):
        return pltpu.make_async_remote_copy(
            src_ref=kv.at[slot],
            dst_ref=kv.at[slot],
            send_sem=kv_send.at[0],
            recv_sem=kv_recv.at[slot],
            device_id=chip(0, 0, 0, sib),
            device_id_type=MESH,
        )

    to_sib = pltpu.make_async_remote_copy(
        src_ref=other, dst_ref=kv.at[c], send_sem=sib_send, recv_sem=kv_recv.at[c],
        device_id=chip(0, 0, 0, sib), device_id_type=MESH,
    )
    to_sib.start()
    q_out = pltpu.make_async_remote_copy(
        src_ref=q_hbm.at[:, pl.ds(pl.multiple_of(sib * wide, wide), wide)],
        dst_ref=qraw.at[c],
        send_sem=q_send,
        recv_sem=q_recv,
        device_id=chip(0, 0, 0, sib),
        device_id_type=MESH,
    )
    q_out.start()
    for n in range(4):
        first_copy(n, c).start()
    arrival(sib).wait_recv()
    for n in range(4):
        first_copy(n, sib).start()

    lane = lax.broadcasted_iota(jnp.int32, (16, HD), 1)
    own = jnp.zeros((16, HD), jnp.float32)
    for run in range(4):
        at = 2 * ROWS + 16 * (run % 2)
        own = jnp.where(lane == run, kv[run // 2, at : at + 16, :].astype(jnp.float32), own)

    def fill_bias(slot):
        for run in range(2):
            block = kv[slot, 2 * ROWS + 16 * run : 2 * ROWS + 16 * run + 16, :].astype(jnp.float32)
            tile = jnp.where(block < own, 0.0, HIDDEN).astype(jnp.bfloat16)
            for r in range(8):
                bias[slot, run * HD + 16 * r : run * HD + 16 * r + 16, :] = tile

    q_mine.wait()
    q_in = pltpu.make_async_remote_copy(
        src_ref=qraw.at[sib], dst_ref=qraw.at[sib], send_sem=q_send, recv_sem=q_recv,
        device_id=chip(0, 0, 0, sib), device_id_type=MESH,
    )
    q_in.wait_recv()
    scale = 1.4426950408889634 / HD**0.5
    lanes = lax.broadcasted_iota(jnp.int32, (TILE, HD), 1)
    row = lax.rem(lax.broadcasted_iota(jnp.int32, (TILE, HD), 0), PART)

    def begin(tile, carry):
        shard, part = tile // 8, lax.rem(tile, 8)
        rows = pl.ds(pl.multiple_of(part * PART, PART), PART)
        for h in range(GROUP):
            piece = qraw[shard, rows, h * HD : (h + 1) * HD].astype(jnp.float32) * scale
            qx[tile, h * PART : (h + 1) * PART, :HD] = piece.astype(jnp.bfloat16)
        qx[tile, :, HD:] = jnp.where(lanes == 2 * shard + part // 4, 1.0, 0.0).astype(jnp.bfloat16)
        top[tile] = jnp.full((TILE, HD), HIDDEN, jnp.float32)
        acc[tile] = jnp.zeros((TILE, 2 * HD), jnp.float32)
        return carry

    def slots_of(places):
        return [2 * place + half for place in places for half in range(2)]

    def pair(slots):
        k = jnp.concatenate([kv[slot, :ROWS, :] for slot in slots], axis=0)
        b = jnp.concatenate([bias[slot] for slot in slots], axis=0)
        v = jnp.concatenate([kv[slot, ROWS : 2 * ROWS, :] for slot in slots], axis=0)
        return jnp.concatenate([k, b], axis=1), v

    for slot in range(2):
        fill_bias(slot)
    lax.fori_loop(0, TILES, begin, 0, unroll=2)

    scores, weights, fades = (s_even, s_odd), (p_even, p_odd), (f_even, f_odd)

    def score(tile, slots, b):
        k, _ = pair(slots)
        scores[b][:, : ROWS * len(slots)] = dot_nt(qx[tile], k)

    def weigh(tile, keys, b):
        s = scores[b][:, :keys]
        before = top[tile]
        high = jnp.maximum(before, jnp.max(s, axis=1, keepdims=True))
        weights[b][:, :keys] = jnp.exp2(s - high[:, :1]).astype(jnp.bfloat16)
        fades[b][...] = jnp.exp2(before - high)
        top[tile] = high

    def add(tile, v, b):
        fade = fades[b][...]
        acc[tile] = acc[tile] * jnp.concatenate([fade, fade], axis=1) + dot(
            weights[b][:, : v.shape[0]], jnp.concatenate([v, jnp.ones_like(v)], axis=1)
        )

    def gather(tile, slots, b):
        add(tile, pair(slots)[1], b)

    def score_own(tile, b):
        shard, part = tile // 8, lax.rem(tile, 8)
        keys = pl.ds(pl.multiple_of(part // 4 * HD, HD), HD)
        diag = dot_nt(qx[tile, :, :HD], kv[shard, keys, :])
        scores[b][:, :HD] = jnp.where(lanes <= row + lax.rem(part, 4) * PART, diag, HIDDEN)
        scores[b][:, HD : HD + 2 * ROWS] = dot_nt(qx[tile], pair([0, 1])[0])

    def gather_own(tile, b):
        vals = pl.ds(pl.multiple_of(ROWS + lax.rem(tile, 8) // 4 * HD, HD), HD)
        add(tile, jnp.concatenate([kv[tile // 8, vals, :], pair([0, 1])[1]], axis=0), b)

    def nothing_before():
        weights[1][...] = jnp.zeros_like(weights[1])
        fades[1][...] = jnp.ones_like(fades[1])

    def own_turn(turn, carry):
        for u in range(BAND):
            tile = turn * BAND + u
            score_own(jnp.minimum(tile + 1, TILES - 1), (u + 1) % 2)
            gather_own(jnp.maximum(tile - 1, 0), (u + 1) % 2)
            weigh(tile, HD + 2 * ROWS, u % 2)
        return carry

    nothing_before()
    score_own(0, 0)
    lax.fori_loop(0, 2, own_turn, 0)
    gather_own(TILES - 1, 1)

    def serve(places, halves=(0, 1)):
        for place in places:
            for half in halves:
                arrival(2 * place + half).wait_recv()
                for index, send in enumerate(SENDS):
                    if send[:2] == (place, half) and (place > 4 or send[4] not in LATER):
                        kv_copy(index).start()
                fill_bias(2 * place + half)

    def send_later(half):
        for index, send in enumerate(SENDS):
            if 0 < send[0] < 5 and send[1] == half and send[4] in LATER:
                kv_copy(index).start()

    def slots_at(turn):
        step = turn // 2
        half = jnp.where(lax.rem(step, 2) == 0, c, sib)
        start = jnp.where(step < 4, 2 + 8 * (step // 2) + half, 4 * step + 2)
        stride = jnp.where(step < 4, 2, 1)
        return [start + stride * a for a in range(4)]

    def tile_at(turn, u):
        return lax.rem(turn, 2) * BAND + u

    for core in range(2):

        @pl.when(c == core)
        def _():
            serve((1, 2, 3, 4), (core,))

    score(0, slots_at(0), 0)

    def early(turn, carry):
        for i in sorted({entry[0] for entry in SERVED} | {1, 2}):

            @pl.when(turn == i)
            def _():
                for when, places, which in SERVED:
                    if when == i and which == 2:
                        serve(places)
                for core in range(2):

                    @pl.when(c == core)
                    def _():
                        for when, places, which in SERVED:
                            if when == i and which < 2:
                                serve(places, ((core + which) % 2,))
                        if i < 3:
                            send_later((core + i + 1) % 2)

        here = slots_at(turn)
        before = slots_at(jnp.maximum(turn - 1, 0))
        after = slots_at(jnp.minimum(turn + 1, 2 * STEPS - 1))
        for u in range(BAND):
            now, other_one = u % 2, (u + 1) % 2
            if u + 1 < BAND:
                score(tile_at(turn, u + 1), here, other_one)
            else:
                score(tile_at(turn + 1, 0), after, other_one)
            if u:
                gather(tile_at(turn, u - 1), here, other_one)
            else:
                gather(tile_at(turn + 1, BAND - 1), before, other_one)
            weigh(tile_at(turn, u), 4 * ROWS, now)
        return carry

    nothing_before()
    lax.fori_loop(0, 2 * STEPS, early, 0)
    gather(TILES - 1, slots_at(2 * STEPS - 1), 1)
    serve((15,))

    def landing(half, source):
        cols = pl.ds(pl.multiple_of(source * wide, wide), wide)
        return att.at[pl.ds(pl.multiple_of(half * PART, PART), PART), cols]

    def own_copy(half):
        return pltpu.make_async_copy(
            obuf.at[c * 8 + x * 2 + half], landing(half, 2 * x + c), out_sem.at[half]
        )

    def place_of(g, u):
        middle = (g == 1) | (g == 2)
        dx = jnp.where(middle, 1 + 2 * (u // 2), jnp.where(g == 0, 2, 0))
        return dx, lax.rem(jnp.where(middle, c + g, c + 1 + u // 2), 2), u % 2

    def tile_of(g, u):
        dx, shard, half = place_of(g, u)
        return shard * 8 + lax.rem(x + dx, 4) * 2 + half

    def att_copy(g, u):
        dx, shard, half = place_of(g, u)
        tile = tile_of(g, u)
        return pltpu.make_async_remote_copy(
            src_ref=obuf.at[tile],
            dst_ref=landing(half, 2 * x + c),
            send_sem=att_send.at[tile],
            recv_sem=att_recv.at[half, 2 * x + c],
            device_id=chip(dx, 0, 0, shard),
            device_id_type=MESH,
        )

    def sib_copy(half):
        tile = sib * 8 + x * 2 + half
        return pltpu.make_async_remote_copy(
            src_ref=obuf.at[tile],
            dst_ref=landing(half, 2 * x + c),
            send_sem=att_send.at[tile],
            recv_sem=att_recv.at[half, 2 * x + c],
            device_id=chip(0, 0, 0, sib),
            device_id_type=MESH,
        )

    last = slots_of(LAST)

    def finish(g, more):
        for u in range(4):
            if u < 3:
                score(tile_of(g, u + 1), last, (u + 1) % 2)
            elif more:
                score(tile_of(g + 1, 0), last, 0)
            if u:
                gather(tile_of(g, u - 1), last, (u + 1) % 2)
            weigh(tile_of(g, u), len(last) * ROWS, u % 2)
        gather(tile_of(g, 3), last, 1)
        for u in range(4):
            tile = tile_of(g, u)
            total = acc[tile]
            o = (total[:, :HD] / total[:, HD:]).astype(jnp.bfloat16)
            for h in range(GROUP):
                obuf[tile, :, h * HD : (h + 1) * HD] = o[h * PART : (h + 1) * PART, :]

    def finish_and_send(g, carry):
        finish(g, True)
        for u in range(4):
            att_copy(g, u).start()
        return carry

    score(tile_of(0, 0), last, 0)
    lax.fori_loop(0, 3, finish_and_send, 0)
    finish(3, False)
    for half in range(2):
        sib_copy(half).start()
        own_copy(half).start()
    for half in range(2):
        for n in range(1, 8):
            source = lax.rem(2 * x + c + n, 8)
            pltpu.make_async_remote_copy(
                src_ref=landing(half, source), dst_ref=landing(half, source), send_sem=q_send,
                recv_sem=att_recv.at[half, source], device_id=chip(0, 0, 0, sib), device_id_type=MESH,
            ).wait_recv()
    to_sib.wait_send()
    q_out.wait_send()
    for n in range(4):
        for half in range(2):
            first_copy(n, half).wait_send()
    for index in range(len(FIRST), len(SENDS)):
        kv_copy(index).wait_send()

    def sent(g, carry):
        for u in range(4):
            att_copy(g, u).wait_send()
        return carry

    lax.fori_loop(0, 3, sent, 0)
    for half in range(2):
        sib_copy(half).wait_send()
    for half in range(2):
        own_copy(half).wait()


def per_device(queries, keys, values, positions, residual, gain):
    width = residual.shape[2]
    rows = residual.shape[1]
    hbm = pl.BlockSpec(memory_space=pl.ANY)
    vmem = pl.BlockSpec(memory_space=pltpu.VMEM)
    dma = pltpu.SemaphoreType.DMA
    bf16, f32 = jnp.bfloat16, jnp.float32
    attended = pl.pallas_call(
        kernel,
        out_shape=jax.ShapeDtypeStruct((rows, width), bf16),
        in_specs=[vmem, hbm, hbm, hbm],
        out_specs=hbm,
        scratch_shapes=[
            pltpu.VMEM((32, MSG, HD), bf16),
            pltpu.VMEM((MSG, HD), bf16),
            pltpu.VMEM((32, ROWS, HD), bf16),
            pltpu.VMEM((2, ROWS, GROUP * HD), bf16),
            pltpu.VMEM((TILES, TILE, 2 * HD), bf16),
            pltpu.VMEM((TILES, TILE, HD), f32),
            pltpu.VMEM((TILES, TILE, 2 * HD), f32),
            pltpu.VMEM((TILES, PART, GROUP * HD), bf16),
            pltpu.VMEM((TILE, 10 * ROWS), f32),
            pltpu.VMEM((TILE, 10 * ROWS), f32),
            pltpu.VMEM((TILE, 10 * ROWS), bf16),
            pltpu.VMEM((TILE, 10 * ROWS), bf16),
            pltpu.VMEM((TILE, HD), f32),
            pltpu.VMEM((TILE, HD), f32),
            dma((5,)),
            dma((len(SENDS),)),
            dma((32,)),
            dma,
            dma,
            dma,
            dma((TILES,)),
            dma((2, 8)),
            dma((2,)),
        ],
        compiler_params=pltpu.CompilerParams(
            collective_id=0, has_side_effects=True, vmem_limit_bytes=60 * 2**20
        ),
    )(positions.reshape(2, HD), queries, keys, values)
    stream = residual[0] + attended.astype(f32)
    inv = lax.rsqrt(jnp.mean(stream * stream, axis=1, keepdims=True) + 1e-05)
    normed = (stream * inv * gain).astype(bf16)
    return (stream[None], normed[None])


def solution(mesh):
    both = ("outer", "inner")
    return jax.shard_map(
        per_device,
        mesh=mesh,
        in_specs=(P(both, "head"), P(both, "head"), P(both, "head"), P(both), P(both, "head", None), P()),
        out_specs=(P(both, "head", None), P(both, "head", None)),
        check_vma=False,
    )
```

```python
import jax
import jax.numpy as jnp
from jax import lax
from jax.experimental import pallas as pl
from jax.experimental.pallas import tpu as pltpu
from jax.sharding import PartitionSpec as P

HD = 128
ROWS = 256
GROUP = 8
PART = 32
TILES = 16
TILE = GROUP * PART
MSG = 2 * ROWS + 32
STEPS = 5
HIDDEN = -1e30
MESH = pl.DeviceIdType.MESH

PLACES = [(0, 0), (1, 0), (3, 0), (0, 1), (0, 3), (2, 0), (0, 2),
          (1, 1), (1, 3), (3, 1), (3, 3), (2, 1), (2, 3), (1, 2), (3, 2), (2, 2)]

SERVED = [(1, (1, 2, 3, 4), 1), (3, (5, 6, 7, 8), 0), (4, (9, 10), 0), (5, (5, 6, 7, 8), 1), (6, (9, 10), 1),
          (8, (11, 14), 2), (9, (12, 13), 2)]
LATER = (9, 10)
LAST = (11, 12, 13, 14, 15)
BAND = TILES // 2


def dot(a, b):
    return jnp.dot(a, b, preferred_element_type=jnp.float32)


def dot_nt(a, b):
    return lax.dot_general(a, b, (((1,), (1,)), ((), ())), preferred_element_type=jnp.float32)


def forwards(place):
    out = []
    here = PLACES[place]
    for half in range(2):
        a, b = here if half == 0 else here[::-1]
        there = []
        if a == 0 and b == 0:
            there += [(1, 0), (3, 0)]
        if a == (1, 3)[half] and b == 0:
            there.append((2, 0))
        if b == 0:
            there += [(a, 1), (a, 3)]
        if b == (1 if a in ((0, 2, 3), (3,))[half] else 3):
            there.append((a, 2))
        for na, nb in there:
            da, db = (na - a) % 4, (nb - b) % 4
            step, new = ((da, db), (na, nb)) if half == 0 else ((db, da), (nb, na))
            out.append((half,) + step + (PLACES.index(new),))
    return out


FIRST = forwards(0)
SENDS = [(j,) + f for j in range(16) for f in forwards(j)]
AROUND = [(1, 0), (3, 0), (0, 1), (0, 3)]


def kernel(
    pos_ref, q_hbm, k_hbm, v_hbm, att,
    kv, other, bias, qraw, qx, top, acc, obuf, s_even, s_odd, p_even, p_odd, f_even, f_odd,
    stage_sem, kv_send, kv_recv, q_send, q_recv, sib_send, att_send, att_recv, out_sem,
):
    x = lax.axis_index("head")
    outer = lax.axis_index("outer")
    inner = lax.axis_index("inner")
    y_hi, z = outer // 4, lax.rem(outer, 4)
    y_lo, c = inner // 2, lax.rem(inner, 2)
    y = y_hi * 2 + y_lo
    sib = 1 - c

    def chip(dx, dz, dy, core):
        zz, yy = lax.rem(z + dz, 4), lax.rem(y + dy, 4)
        return (lax.rem(x + dx, 4), (yy // 2) * 4 + zz, lax.rem(yy, 2) * 2 + core)

    mine = pl.ds(pl.multiple_of(c * HD, HD), HD)
    theirs = pl.ds(pl.multiple_of(sib * HD, HD), HD)
    stage = [
        pltpu.make_async_copy(k_hbm.at[:, mine], kv.at[c, pl.ds(0, ROWS)], stage_sem.at[0]),
        pltpu.make_async_copy(v_hbm.at[:, mine], kv.at[c, pl.ds(ROWS, ROWS)], stage_sem.at[1]),
        pltpu.make_async_copy(k_hbm.at[:, theirs], other.at[pl.ds(0, ROWS)], stage_sem.at[2]),
        pltpu.make_async_copy(v_hbm.at[:, theirs], other.at[pl.ds(ROWS, ROWS)], stage_sem.at[3]),
    ]
    for copy in stage:
        copy.start()
    wide = GROUP * HD
    q_mine = pltpu.make_async_copy(
        q_hbm.at[:, pl.ds(pl.multiple_of(c * wide, wide), wide)], qraw.at[c], stage_sem.at[4]
    )
    q_mine.start()

    partners = [chip(0, 0, 0, sib)]
    partners += [chip(0, dz, dy, c) for dz, dy in AROUND]
    partners += [chip(dx, 0, 0, core) for dx in (1, 2, 3) for core in (c, sib)]
    barrier = pltpu.get_barrier_semaphore()
    for partner in partners:
        pl.semaphore_signal(barrier, inc=1, device_id=partner, device_id_type=MESH)

    for run in range(2):
        block = (pos_ref[run : run + 1, :] >> 7).astype(jnp.float32)
        tile = jnp.broadcast_to(block, (16, HD)).astype(jnp.bfloat16)
        kv[c, 2 * ROWS + 16 * run : 2 * ROWS + 16 * run + 16, :] = tile
        other[2 * ROWS + 16 * run : 2 * ROWS + 16 * run + 16, :] = tile
    for copy in stage:
        copy.wait()
    pl.semaphore_wait(barrier, len(partners))

    def kv_copy(index):
        place, half, dz, dy, there = SENDS[index]
        return pltpu.make_async_remote_copy(
            src_ref=kv.at[2 * place + half],
            dst_ref=kv.at[2 * there + half],
            send_sem=kv_send.at[index],
            recv_sem=kv_recv.at[2 * there + half],
            device_id=chip(0, dz, dy, c),
            device_id_type=MESH,
        )

    def first_copy(n, half):
        dz, dy = AROUND[n]
        return pltpu.make_async_remote_copy(
            src_ref=kv.at[half],
            dst_ref=kv.at[2 * (1 + n) + half],
            send_sem=kv_send.at[2 * n + half],
            recv_sem=kv_recv.at[2 * (1 + n) + half],
            device_id=chip(0, dz, dy, c),
            device_id_type=MESH,
        )

    def arrival(slot):
        return pltpu.make_async_remote_copy(
            src_ref=kv.at[slot],
            dst_ref=kv.at[slot],
            send_sem=kv_send.at[0],
            recv_sem=kv_recv.at[slot],
            device_id=chip(0, 0, 0, sib),
            device_id_type=MESH,
        )

    to_sib = pltpu.make_async_remote_copy(
        src_ref=other, dst_ref=kv.at[c], send_sem=sib_send, recv_sem=kv_recv.at[c],
        device_id=chip(0, 0, 0, sib), device_id_type=MESH,
    )
    to_sib.start()
    q_out = pltpu.make_async_remote_copy(
        src_ref=q_hbm.at[:, pl.ds(pl.multiple_of(sib * wide, wide), wide)],
        dst_ref=qraw.at[c],
        send_sem=q_send,
        recv_sem=q_recv,
        device_id=chip(0, 0, 0, sib),
        device_id_type=MESH,
    )
    q_out.start()
    for n in range(4):
        first_copy(n, c).start()
    arrival(sib).wait_recv()
    for n in range(4):
        first_copy(n, sib).start()

    lane = lax.broadcasted_iota(jnp.int32, (16, HD), 1)
    own = jnp.zeros((16, HD), jnp.float32)
    for run in range(4):
        at = 2 * ROWS + 16 * (run % 2)
        own = jnp.where(lane == run, kv[run // 2, at : at + 16, :].astype(jnp.float32), own)

    def fill_bias(slot):
        for run in range(2):
            block = kv[slot, 2 * ROWS + 16 * run : 2 * ROWS + 16 * run + 16, :].astype(jnp.float32)
            tile = jnp.where(block < own, 0.0, HIDDEN).astype(jnp.bfloat16)
            for r in range(8):
                bias[slot, run * HD + 16 * r : run * HD + 16 * r + 16, :] = tile

    q_mine.wait()
    q_in = pltpu.make_async_remote_copy(
        src_ref=qraw.at[sib], dst_ref=qraw.at[sib], send_sem=q_send, recv_sem=q_recv,
        device_id=chip(0, 0, 0, sib), device_id_type=MESH,
    )
    q_in.wait_recv()
    scale = 1.4426950408889634 / HD**0.5
    lanes = lax.broadcasted_iota(jnp.int32, (TILE, HD), 1)
    row = lax.rem(lax.broadcasted_iota(jnp.int32, (TILE, HD), 0), PART)

    def begin(tile, carry):
        shard, part = tile // 8, lax.rem(tile, 8)
        rows = pl.ds(pl.multiple_of(part * PART, PART), PART)
        for h in range(GROUP):
            piece = qraw[shard, rows, h * HD : (h + 1) * HD].astype(jnp.float32) * scale
            qx[tile, h * PART : (h + 1) * PART, :HD] = piece.astype(jnp.bfloat16)
        qx[tile, :, HD:] = jnp.where(lanes == 2 * shard + part // 4, 1.0, 0.0).astype(jnp.bfloat16)
        top[tile] = jnp.full((TILE, HD), HIDDEN, jnp.float32)
        acc[tile] = jnp.zeros((TILE, 2 * HD), jnp.float32)
        return carry

    def slots_of(places):
        return [2 * place + half for place in places for half in range(2)]

    def pair(slots):
        k = jnp.concatenate([kv[slot, :ROWS, :] for slot in slots], axis=0)
        b = jnp.concatenate([bias[slot] for slot in slots], axis=0)
        v = jnp.concatenate([kv[slot, ROWS : 2 * ROWS, :] for slot in slots], axis=0)
        return jnp.concatenate([k, b], axis=1), v

    for slot in range(2):
        fill_bias(slot)
    lax.fori_loop(0, TILES, begin, 0, unroll=2)

    scores, weights, fades = (s_even, s_odd), (p_even, p_odd), (f_even, f_odd)

    def score(tile, slots, b):
        k, _ = pair(slots)
        scores[b][:, : ROWS * len(slots)] = dot_nt(qx[tile], k)

    def weigh(tile, keys, b):
        s = scores[b][:, :keys]
        before = top[tile]
        high = jnp.maximum(before, jnp.max(s, axis=1, keepdims=True))
        weights[b][:, :keys] = jnp.exp2(s - high[:, :1]).astype(jnp.bfloat16)
        fades[b][...] = jnp.exp2(before - high)
        top[tile] = high

    def add(tile, v, b):
        fade = fades[b][...]
        acc[tile] = acc[tile] * jnp.concatenate([fade, fade], axis=1) + dot(
            weights[b][:, : v.shape[0]], jnp.concatenate([v, jnp.ones_like(v)], axis=1)
        )

    def gather(tile, slots, b):
        add(tile, pair(slots)[1], b)

    def score_own(tile, b):
        shard, part = tile // 8, lax.rem(tile, 8)
        keys = pl.ds(pl.multiple_of(part // 4 * HD, HD), HD)
        diag = dot_nt(qx[tile, :, :HD], kv[shard, keys, :])
        scores[b][:, :HD] = jnp.where(lanes <= row + lax.rem(part, 4) * PART, diag, HIDDEN)
        scores[b][:, HD : HD + 2 * ROWS] = dot_nt(qx[tile], pair([0, 1])[0])

    def gather_own(tile, b):
        vals = pl.ds(pl.multiple_of(ROWS + lax.rem(tile, 8) // 4 * HD, HD), HD)
        add(tile, jnp.concatenate([kv[tile // 8, vals, :], pair([0, 1])[1]], axis=0), b)

    def nothing_before():
        weights[1][...] = jnp.zeros_like(weights[1])
        fades[1][...] = jnp.ones_like(fades[1])

    def own_turn(turn, carry):
        for u in range(BAND):
            tile = turn * BAND + u
            score_own(jnp.minimum(tile + 1, TILES - 1), (u + 1) % 2)
            gather_own(jnp.maximum(tile - 1, 0), (u + 1) % 2)
            weigh(tile, HD + 2 * ROWS, u % 2)
        return carry

    nothing_before()
    score_own(0, 0)
    lax.fori_loop(0, 2, own_turn, 0)
    gather_own(TILES - 1, 1)

    def serve(places, halves=(0, 1)):
        for place in places:
            for half in halves:
                arrival(2 * place + half).wait_recv()
                for index, send in enumerate(SENDS):
                    if send[:2] == (place, half) and (place > 4 or send[4] not in LATER):
                        kv_copy(index).start()
                fill_bias(2 * place + half)

    def send_later(half):
        for index, send in enumerate(SENDS):
            if 0 < send[0] < 5 and send[1] == half and send[4] in LATER:
                kv_copy(index).start()

    def slots_at(turn):
        step = turn // 2
        half = jnp.where(lax.rem(step, 2) == 0, c, sib)
        start = jnp.where(step < 4, 2 + 8 * (step // 2) + half, 4 * step + 2)
        stride = jnp.where(step < 4, 2, 1)
        return [start + stride * a for a in range(4)]

    def tile_at(turn, u):
        return lax.rem(turn, 2) * BAND + u

    for core in range(2):

        @pl.when(c == core)
        def _():
            serve((1, 2, 3, 4), (core,))

    score(0, slots_at(0), 0)

    def early(turn, carry):
        for i in sorted({entry[0] for entry in SERVED} | {1, 2}):

            @pl.when(turn == i)
            def _():
                for when, places, which in SERVED:
                    if when == i and which == 2:
                        serve(places)
                for core in range(2):

                    @pl.when(c == core)
                    def _():
                        for when, places, which in SERVED:
                            if when == i and which < 2:
                                serve(places, ((core + which) % 2,))
                        if i < 3:
                            send_later((core + i + 1) % 2)

        here = slots_at(turn)
        before = slots_at(jnp.maximum(turn - 1, 0))
        after = slots_at(jnp.minimum(turn + 1, 2 * STEPS - 1))
        for u in range(BAND):
            now, other_one = u % 2, (u + 1) % 2
            if u + 1 < BAND:
                score(tile_at(turn, u + 1), here, other_one)
            else:
                score(tile_at(turn + 1, 0), after, other_one)
            if u:
                gather(tile_at(turn, u - 1), here, other_one)
            else:
                gather(tile_at(turn + 1, BAND - 1), before, other_one)
            weigh(tile_at(turn, u), 4 * ROWS, now)
        return carry

    nothing_before()
    lax.fori_loop(0, 2 * STEPS, early, 0)
    gather(TILES - 1, slots_at(2 * STEPS - 1), 1)
    serve((15,))

    def landing(half, source):
        cols = pl.ds(pl.multiple_of(source * wide, wide), wide)
        return att.at[pl.ds(pl.multiple_of(half * PART, PART), PART), cols]

    def own_copy(half):
        return pltpu.make_async_copy(
            obuf.at[c * 8 + x * 2 + half], landing(half, 2 * x + c), out_sem.at[half]
        )

    def place_of(g, u):
        middle = g in (1, 2)
        dx = 1 + 2 * (u // 2) if middle else 2 if g == 0 else 0
        return dx, lax.rem(c + g if middle else c + 1 + u // 2, 2), u % 2

    def tile_of(g, u):
        dx, shard, half = place_of(g, u)
        return shard * 8 + lax.rem(x + dx, 4) * 2 + half

    def att_copy(g, u):
        dx, shard, half = place_of(g, u)
        tile = tile_of(g, u)
        return pltpu.make_async_remote_copy(
            src_ref=obuf.at[tile],
            dst_ref=landing(half, 2 * x + c),
            send_sem=att_send.at[tile],
            recv_sem=att_recv.at[half, 2 * x + c],
            device_id=chip(dx, 0, 0, shard),
            device_id_type=MESH,
        )

    def sib_copy(half):
        tile = sib * 8 + x * 2 + half
        return pltpu.make_async_remote_copy(
            src_ref=obuf.at[tile],
            dst_ref=landing(half, 2 * x + c),
            send_sem=att_send.at[tile],
            recv_sem=att_recv.at[half, 2 * x + c],
            device_id=chip(0, 0, 0, sib),
            device_id_type=MESH,
        )

    last = slots_of(LAST)

    def deliver(g, pair_of):
        for u in pair_of:
            tile = tile_of(g, u)
            total = acc[tile]
            o = (total[:, :HD] / total[:, HD:]).astype(jnp.bfloat16)
            for h in range(GROUP):
                obuf[tile, :, h * HD : (h + 1) * HD] = o[h * PART : (h + 1) * PART, :]
        for u in pair_of:
            if g < 3:
                att_copy(g, u).start()
            elif u < 2:
                sib_copy(u).start()
            else:
                own_copy(u - 2).start()

    score(tile_of(0, 0), last, 0)
    for i in range(16):
        if i < 15:
            score(tile_of((i + 1) // 4, (i + 1) % 4), last, (i + 1) % 2)
        if i:
            gather(tile_of((i - 1) // 4, (i - 1) % 4), last, (i + 1) % 2)
        weigh(tile_of(i // 4, i % 4), len(last) * ROWS, i % 2)
        if i and i % 2 == 0:
            deliver((i - 2) // 4, (0, 1) if i % 4 == 2 else (2, 3))
    gather(tile_of(3, 3), last, 1)
    deliver(3, (2, 3))
    for half in range(2):
        for n in range(1, 8):
            source = lax.rem(2 * x + c + n, 8)
            pltpu.make_async_remote_copy(
                src_ref=landing(half, source), dst_ref=landing(half, source), send_sem=q_send,
                recv_sem=att_recv.at[half, source], device_id=chip(0, 0, 0, sib), device_id_type=MESH,
            ).wait_recv()
    to_sib.wait_send()
    q_out.wait_send()
    for n in range(4):
        for half in range(2):
            first_copy(n, half).wait_send()
    for index in range(len(FIRST), len(SENDS)):
        kv_copy(index).wait_send()

    for g in range(3):
        for u in range(4):
            att_copy(g, u).wait_send()
    for half in range(2):
        sib_copy(half).wait_send()
    for half in range(2):
        own_copy(half).wait()


def per_device(queries, keys, values, positions, residual, gain):
    width = residual.shape[2]
    rows = residual.shape[1]
    hbm = pl.BlockSpec(memory_space=pl.ANY)
    vmem = pl.BlockSpec(memory_space=pltpu.VMEM)
    dma = pltpu.SemaphoreType.DMA
    bf16, f32 = jnp.bfloat16, jnp.float32
    attended = pl.pallas_call(
        kernel,
        out_shape=jax.ShapeDtypeStruct((rows, width), bf16),
        in_specs=[vmem, hbm, hbm, hbm],
        out_specs=hbm,
        scratch_shapes=[
            pltpu.VMEM((32, MSG, HD), bf16),
            pltpu.VMEM((MSG, HD), bf16),
            pltpu.VMEM((32, ROWS, HD), bf16),
            pltpu.VMEM((2, ROWS, GROUP * HD), bf16),
            pltpu.VMEM((TILES, TILE, 2 * HD), bf16),
            pltpu.VMEM((TILES, TILE, HD), f32),
            pltpu.VMEM((TILES, TILE, 2 * HD), f32),
            pltpu.VMEM((TILES, PART, GROUP * HD), bf16),
            pltpu.VMEM((TILE, 10 * ROWS), f32),
            pltpu.VMEM((TILE, 10 * ROWS), f32),
            pltpu.VMEM((TILE, 10 * ROWS), bf16),
            pltpu.VMEM((TILE, 10 * ROWS), bf16),
            pltpu.VMEM((TILE, HD), f32),
            pltpu.VMEM((TILE, HD), f32),
            dma((5,)),
            dma((len(SENDS),)),
            dma((32,)),
            dma,
            dma,
            dma,
            dma((TILES,)),
            dma((2, 8)),
            dma((2,)),
        ],
        compiler_params=pltpu.CompilerParams(
            collective_id=0, has_side_effects=True, vmem_limit_bytes=60 * 2**20
        ),
    )(positions.reshape(2, HD), queries, keys, values)
    stream = residual[0] + attended.astype(f32)
    inv = lax.rsqrt(jnp.mean(stream * stream, axis=1, keepdims=True) + 1e-05)
    normed = (stream * inv * gain).astype(bf16)
    return (stream[None], normed[None])


def solution(mesh):
    both = ("outer", "inner")
    return jax.shard_map(
        per_device,
        mesh=mesh,
        in_specs=(P(both, "head"), P(both, "head"), P(both, "head"), P(both), P(both, "head", None), P()),
        out_specs=(P(both, "head", None), P(both, "head", None)),
        check_vma=False,
    )
```

```python
import jax
import jax.numpy as jnp
from jax import lax
from jax.experimental import pallas as pl
from jax.experimental.pallas import tpu as pltpu
from jax.sharding import PartitionSpec as P

HD = 128
ROWS = 256
GROUP = 8
PART = 32
TILES = 16
TILE = GROUP * PART
MSG = 2 * ROWS + 32
STEPS = 5
HIDDEN = -1e30
MESH = pl.DeviceIdType.MESH

PLACES = [(0, 0), (1, 0), (3, 0), (0, 1), (0, 3), (2, 0), (0, 2),
          (1, 1), (1, 3), (3, 1), (3, 3), (2, 1), (2, 3), (1, 2), (3, 2), (2, 2)]

SERVED = [(1, (1, 2, 3, 4), 1), (3, (5, 6, 7, 8), 0), (4, (9, 10), 0), (5, (5, 6, 7, 8), 1), (6, (9, 10), 1),
          (8, (11, 14), 2), (9, (12, 13), 2)]
LATER = (9, 10)
LAST = (11, 12, 13, 14, 15)
BAND = TILES // 2


def dot(a, b):
    return jnp.dot(a, b, preferred_element_type=jnp.float32)


def dot_nt(a, b):
    return lax.dot_general(a, b, (((1,), (1,)), ((), ())), preferred_element_type=jnp.float32)


def forwards(place):
    out = []
    here = PLACES[place]
    for half in range(2):
        a, b = here if half == 0 else here[::-1]
        there = []
        if a == 0 and b == 0:
            there += [(1, 0), (3, 0)]
        if a == (1, 3)[half] and b == 0:
            there.append((2, 0))
        if b == 0:
            there += [(a, 1), (a, 3)]
        if b == (1 if a in ((0, 2, 3), (3,))[half] else 3):
            there.append((a, 2))
        for na, nb in there:
            da, db = (na - a) % 4, (nb - b) % 4
            step, new = ((da, db), (na, nb)) if half == 0 else ((db, da), (nb, na))
            out.append((half,) + step + (PLACES.index(new),))
    return out


FIRST = forwards(0)
SENDS = [(j,) + f for j in range(16) for f in forwards(j)]
AROUND = [(1, 0), (3, 0), (0, 1), (0, 3)]


def kernel(
    pos_ref, q_hbm, k_hbm, v_hbm, att,
    kv, other, bias, qraw, qx, top, acc, obuf, s_even, s_odd, p_even, p_odd, f_even, f_odd,
    stage_sem, kv_send, kv_recv, q_send, q_recv, sib_send, att_send, att_recv, out_sem,
):
    x = lax.axis_index("head")
    outer = lax.axis_index("outer")
    inner = lax.axis_index("inner")
    y_hi, z = outer // 4, lax.rem(outer, 4)
    y_lo, c = inner // 2, lax.rem(inner, 2)
    y = y_hi * 2 + y_lo
    sib = 1 - c

    def chip(dx, dz, dy, core):
        zz, yy = lax.rem(z + dz, 4), lax.rem(y + dy, 4)
        return (lax.rem(x + dx, 4), (yy // 2) * 4 + zz, lax.rem(yy, 2) * 2 + core)

    mine = pl.ds(pl.multiple_of(c * HD, HD), HD)
    theirs = pl.ds(pl.multiple_of(sib * HD, HD), HD)
    stage = [
        pltpu.make_async_copy(k_hbm.at[:, mine], kv.at[c, pl.ds(0, ROWS)], stage_sem.at[0]),
        pltpu.make_async_copy(v_hbm.at[:, mine], kv.at[c, pl.ds(ROWS, ROWS)], stage_sem.at[1]),
        pltpu.make_async_copy(k_hbm.at[:, theirs], other.at[pl.ds(0, ROWS)], stage_sem.at[2]),
        pltpu.make_async_copy(v_hbm.at[:, theirs], other.at[pl.ds(ROWS, ROWS)], stage_sem.at[3]),
    ]
    for copy in stage:
        copy.start()
    wide = GROUP * HD
    q_mine = pltpu.make_async_copy(
        q_hbm.at[:, pl.ds(pl.multiple_of(c * wide, wide), wide)], qraw.at[c], stage_sem.at[4]
    )
    q_mine.start()

    partners = [chip(0, 0, 0, sib)]
    partners += [chip(0, dz, dy, c) for dz, dy in AROUND]
    partners += [chip(dx, 0, 0, core) for dx in (1, 2, 3) for core in (c, sib)]
    barrier = pltpu.get_barrier_semaphore()
    for partner in partners:
        pl.semaphore_signal(barrier, inc=1, device_id=partner, device_id_type=MESH)

    for run in range(2):
        block = (pos_ref[run : run + 1, :] >> 7).astype(jnp.float32)
        tile = jnp.broadcast_to(block, (16, HD)).astype(jnp.bfloat16)
        kv[c, 2 * ROWS + 16 * run : 2 * ROWS + 16 * run + 16, :] = tile
        other[2 * ROWS + 16 * run : 2 * ROWS + 16 * run + 16, :] = tile
    for copy in stage:
        copy.wait()
    pl.semaphore_wait(barrier, len(partners))

    def kv_copy(index):
        place, half, dz, dy, there = SENDS[index]
        return pltpu.make_async_remote_copy(
            src_ref=kv.at[2 * place + half],
            dst_ref=kv.at[2 * there + half],
            send_sem=kv_send.at[index],
            recv_sem=kv_recv.at[2 * there + half],
            device_id=chip(0, dz, dy, c),
            device_id_type=MESH,
        )

    def first_copy(n, half):
        dz, dy = AROUND[n]
        return pltpu.make_async_remote_copy(
            src_ref=kv.at[half],
            dst_ref=kv.at[2 * (1 + n) + half],
            send_sem=kv_send.at[2 * n + half],
            recv_sem=kv_recv.at[2 * (1 + n) + half],
            device_id=chip(0, dz, dy, c),
            device_id_type=MESH,
        )

    def arrival(slot):
        return pltpu.make_async_remote_copy(
            src_ref=kv.at[slot],
            dst_ref=kv.at[slot],
            send_sem=kv_send.at[0],
            recv_sem=kv_recv.at[slot],
            device_id=chip(0, 0, 0, sib),
            device_id_type=MESH,
        )

    to_sib = pltpu.make_async_remote_copy(
        src_ref=other, dst_ref=kv.at[c], send_sem=sib_send, recv_sem=kv_recv.at[c],
        device_id=chip(0, 0, 0, sib), device_id_type=MESH,
    )
    to_sib.start()
    q_out = pltpu.make_async_remote_copy(
        src_ref=q_hbm.at[:, pl.ds(pl.multiple_of(sib * wide, wide), wide)],
        dst_ref=qraw.at[c],
        send_sem=q_send,
        recv_sem=q_recv,
        device_id=chip(0, 0, 0, sib),
        device_id_type=MESH,
    )
    q_out.start()
    for n in range(4):
        first_copy(n, c).start()
    arrival(sib).wait_recv()
    for n in range(4):
        first_copy(n, sib).start()

    lane = lax.broadcasted_iota(jnp.int32, (16, HD), 1)
    own = jnp.zeros((16, HD), jnp.float32)
    for run in range(4):
        at = 2 * ROWS + 16 * (run % 2)
        own = jnp.where(lane == run, kv[run // 2, at : at + 16, :].astype(jnp.float32), own)

    def fill_bias(slot):
        for run in range(2):
            block = kv[slot, 2 * ROWS + 16 * run : 2 * ROWS + 16 * run + 16, :].astype(jnp.float32)
            tile = jnp.where(block < own, 0.0, HIDDEN).astype(jnp.bfloat16)
            for r in range(8):
                bias[slot, run * HD + 16 * r : run * HD + 16 * r + 16, :] = tile

    q_mine.wait()
    q_in = pltpu.make_async_remote_copy(
        src_ref=qraw.at[sib], dst_ref=qraw.at[sib], send_sem=q_send, recv_sem=q_recv,
        device_id=chip(0, 0, 0, sib), device_id_type=MESH,
    )
    q_in.wait_recv()
    scale = 1.4426950408889634 / HD**0.5
    lanes = lax.broadcasted_iota(jnp.int32, (TILE, HD), 1)
    row = lax.rem(lax.broadcasted_iota(jnp.int32, (TILE, HD), 0), PART)

    def begin(tile, carry):
        shard, part = tile // 8, lax.rem(tile, 8)
        rows = pl.ds(pl.multiple_of(part * PART, PART), PART)
        for h in range(GROUP):
            piece = qraw[shard, rows, h * HD : (h + 1) * HD].astype(jnp.float32) * scale
            qx[tile, h * PART : (h + 1) * PART, :HD] = piece.astype(jnp.bfloat16)
        qx[tile, :, HD:] = jnp.where(lanes == 2 * shard + part // 4, 1.0, 0.0).astype(jnp.bfloat16)
        return carry

    def slots_of(places):
        return [2 * place + half for place in places for half in range(2)]

    def pair(slots):
        k = jnp.concatenate([kv[slot, :ROWS, :] for slot in slots], axis=0)
        b = jnp.concatenate([bias[slot] for slot in slots], axis=0)
        v = jnp.concatenate([kv[slot, ROWS : 2 * ROWS, :] for slot in slots], axis=0)
        return jnp.concatenate([k, b], axis=1), v

    for slot in range(2):
        fill_bias(slot)
    lax.fori_loop(0, TILES, begin, 0, unroll=2)

    scores, weights, fades = (s_even, s_odd), (p_even, p_odd), (f_even, f_odd)

    def score(tile, slots, b):
        k, _ = pair(slots)
        scores[b][:, : ROWS * len(slots)] = dot_nt(qx[tile], k)

    def weigh(tile, keys, b):
        s = scores[b][:, :keys]
        before = top[tile]
        high = jnp.maximum(before, jnp.max(s, axis=1, keepdims=True))
        weights[b][:, :keys] = jnp.exp2(s - high[:, :1]).astype(jnp.bfloat16)
        fades[b][...] = jnp.exp2(before - high)
        top[tile] = high

    def add(tile, v, b):
        fade = fades[b][...]
        acc[tile] = acc[tile] * jnp.concatenate([fade, fade], axis=1) + dot(
            weights[b][:, : v.shape[0]], jnp.concatenate([v, jnp.ones_like(v)], axis=1)
        )

    def gather(tile, slots, b):
        add(tile, pair(slots)[1], b)

    def score_own(tile, b):
        shard, part = tile // 8, lax.rem(tile, 8)
        keys = pl.ds(pl.multiple_of(part // 4 * HD, HD), HD)
        diag = dot_nt(qx[tile, :, :HD], kv[shard, keys, :])
        scores[b][:, :HD] = jnp.where(lanes <= row + lax.rem(part, 4) * PART, diag, HIDDEN)
        scores[b][:, HD : HD + 2 * ROWS] = dot_nt(qx[tile], pair([0, 1])[0])

    def gather_own(tile, b):
        vals = pl.ds(pl.multiple_of(ROWS + lax.rem(tile, 8) // 4 * HD, HD), HD)
        v = jnp.concatenate([kv[tile // 8, vals, :], pair([0, 1])[1]], axis=0)
        acc[tile] = dot(
            weights[b][:, : v.shape[0]], jnp.concatenate([v, jnp.ones_like(v)], axis=1)
        )

    def weigh_own(tile, keys, b):
        s = scores[b][:, :keys]
        high = jnp.broadcast_to(jnp.max(s, axis=1, keepdims=True), (TILE, HD))
        weights[b][:, :keys] = jnp.exp2(s - high[:, :1]).astype(jnp.bfloat16)
        top[tile] = high

    def nothing_before():
        weights[1][...] = jnp.zeros_like(weights[1])
        fades[1][...] = jnp.ones_like(fades[1])

    def own_turn(turn, carry):
        for u in range(BAND):
            tile = turn * BAND + u
            score_own(jnp.minimum(tile + 1, TILES - 1), (u + 1) % 2)
            gather_own(jnp.maximum(tile - 1, 0), (u + 1) % 2)
            weigh_own(tile, HD + 2 * ROWS, u % 2)
        return carry

    nothing_before()
    score_own(0, 0)
    lax.fori_loop(0, 2, own_turn, 0)
    gather_own(TILES - 1, 1)

    def serve(places, halves=(0, 1)):
        for place in places:
            for half in halves:
                arrival(2 * place + half).wait_recv()
                for index, send in enumerate(SENDS):
                    if send[:2] == (place, half) and (place > 4 or send[4] not in LATER):
                        kv_copy(index).start()
                fill_bias(2 * place + half)

    def send_later(half):
        for index, send in enumerate(SENDS):
            if 0 < send[0] < 5 and send[1] == half and send[4] in LATER:
                kv_copy(index).start()

    def slots_at(turn):
        step = turn // 2
        half = jnp.where(lax.rem(step, 2) == 0, c, sib)
        start = jnp.where(step < 4, 2 + 8 * (step // 2) + half, 4 * step + 2)
        stride = jnp.where(step < 4, 2, 1)
        return [start + stride * a for a in range(4)]

    def tile_at(turn, u):
        return lax.rem(turn, 2) * BAND + u

    for core in range(2):

        @pl.when(c == core)
        def _():
            serve((1, 2, 3, 4), (core,))

    score(0, slots_at(0), 0)

    def early(turn, carry):
        for i in sorted({entry[0] for entry in SERVED} | {1, 2}):

            @pl.when(turn == i)
            def _():
                for when, places, which in SERVED:
                    if when == i and which == 2:
                        serve(places)
                for core in range(2):

                    @pl.when(c == core)
                    def _():
                        for when, places, which in SERVED:
                            if when == i and which < 2:
                                serve(places, ((core + which) % 2,))
                        if i < 3:
                            send_later((core + i + 1) % 2)

        here = slots_at(turn)
        before = slots_at(jnp.maximum(turn - 1, 0))
        after = slots_at(jnp.minimum(turn + 1, 2 * STEPS - 1))
        for u in range(BAND):
            now, other_one = u % 2, (u + 1) % 2
            if u + 1 < BAND:
                score(tile_at(turn, u + 1), here, other_one)
            else:
                score(tile_at(turn + 1, 0), after, other_one)
            if u:
                gather(tile_at(turn, u - 1), here, other_one)
            else:
                gather(tile_at(turn + 1, BAND - 1), before, other_one)
            weigh(tile_at(turn, u), 4 * ROWS, now)
        return carry

    nothing_before()
    lax.fori_loop(0, 2 * STEPS, early, 0)
    gather(TILES - 1, slots_at(2 * STEPS - 1), 1)
    serve((15,))

    def landing(half, source):
        cols = pl.ds(pl.multiple_of(source * wide, wide), wide)
        return att.at[pl.ds(pl.multiple_of(half * PART, PART), PART), cols]

    def own_copy(half):
        return pltpu.make_async_copy(
            obuf.at[c * 8 + x * 2 + half], landing(half, 2 * x + c), out_sem.at[half]
        )

    def place_of(g, u):
        middle = g in (1, 2)
        dx = 1 + 2 * (u // 2) if middle else 2 if g == 0 else 0
        return dx, lax.rem(c + g if middle else c + 1 + u // 2, 2), u % 2

    def tile_of(g, u):
        dx, shard, half = place_of(g, u)
        return shard * 8 + lax.rem(x + dx, 4) * 2 + half

    def att_copy(g, u):
        dx, shard, half = place_of(g, u)
        tile = tile_of(g, u)
        return pltpu.make_async_remote_copy(
            src_ref=obuf.at[tile],
            dst_ref=landing(half, 2 * x + c),
            send_sem=att_send.at[tile],
            recv_sem=att_recv.at[half, 2 * x + c],
            device_id=chip(dx, 0, 0, shard),
            device_id_type=MESH,
        )

    def sib_copy(half):
        tile = sib * 8 + x * 2 + half
        return pltpu.make_async_remote_copy(
            src_ref=obuf.at[tile],
            dst_ref=landing(half, 2 * x + c),
            send_sem=att_send.at[tile],
            recv_sem=att_recv.at[half, 2 * x + c],
            device_id=chip(0, 0, 0, sib),
            device_id_type=MESH,
        )

    last = slots_of(LAST)

    def deliver(g, pair_of):
        for u in pair_of:
            tile = tile_of(g, u)
            total = acc[tile]
            o = (total[:, :HD] / total[:, HD:]).astype(jnp.bfloat16)
            for h in range(GROUP):
                obuf[tile, :, h * HD : (h + 1) * HD] = o[h * PART : (h + 1) * PART, :]
        for u in pair_of:
            if g < 3:
                att_copy(g, u).start()
            elif u < 2:
                sib_copy(u).start()
            else:
                own_copy(u - 2).start()

    score(tile_of(0, 0), last, 0)
    for i in range(16):
        if i < 15:
            score(tile_of((i + 1) // 4, (i + 1) % 4), last, (i + 1) % 2)
        if i:
            gather(tile_of((i - 1) // 4, (i - 1) % 4), last, (i + 1) % 2)
        weigh(tile_of(i // 4, i % 4), len(last) * ROWS, i % 2)
        if i and i % 2 == 0:
            deliver((i - 2) // 4, (0, 1) if i % 4 == 2 else (2, 3))
    gather(tile_of(3, 3), last, 1)
    deliver(3, (2, 3))
    for half in range(2):
        for n in range(1, 8):
            source = lax.rem(2 * x + c + n, 8)
            pltpu.make_async_remote_copy(
                src_ref=landing(half, source), dst_ref=landing(half, source), send_sem=q_send,
                recv_sem=att_recv.at[half, source], device_id=chip(0, 0, 0, sib), device_id_type=MESH,
            ).wait_recv()
    to_sib.wait_send()
    q_out.wait_send()
    for n in range(4):
        for half in range(2):
            first_copy(n, half).wait_send()
    for index in range(len(FIRST), len(SENDS)):
        kv_copy(index).wait_send()

    for g in range(3):
        for u in range(4):
            att_copy(g, u).wait_send()
    for half in range(2):
        sib_copy(half).wait_send()
    for half in range(2):
        own_copy(half).wait()


def per_device(queries, keys, values, positions, residual, gain):
    width = residual.shape[2]
    rows = residual.shape[1]
    hbm = pl.BlockSpec(memory_space=pl.ANY)
    vmem = pl.BlockSpec(memory_space=pltpu.VMEM)
    dma = pltpu.SemaphoreType.DMA
    bf16, f32 = jnp.bfloat16, jnp.float32
    attended = pl.pallas_call(
        kernel,
        out_shape=jax.ShapeDtypeStruct((rows, width), bf16),
        in_specs=[vmem, hbm, hbm, hbm],
        out_specs=hbm,
        scratch_shapes=[
            pltpu.VMEM((32, MSG, HD), bf16),
            pltpu.VMEM((MSG, HD), bf16),
            pltpu.VMEM((32, ROWS, HD), bf16),
            pltpu.VMEM((2, ROWS, GROUP * HD), bf16),
            pltpu.VMEM((TILES, TILE, 2 * HD), bf16),
            pltpu.VMEM((TILES, TILE, HD), f32),
            pltpu.VMEM((TILES, TILE, 2 * HD), f32),
            pltpu.VMEM((TILES, PART, GROUP * HD), bf16),
            pltpu.VMEM((TILE, 10 * ROWS), f32),
            pltpu.VMEM((TILE, 10 * ROWS), f32),
            pltpu.VMEM((TILE, 10 * ROWS), bf16),
            pltpu.VMEM((TILE, 10 * ROWS), bf16),
            pltpu.VMEM((TILE, HD), f32),
            pltpu.VMEM((TILE, HD), f32),
            dma((5,)),
            dma((len(SENDS),)),
            dma((32,)),
            dma,
            dma,
            dma,
            dma((TILES,)),
            dma((2, 8)),
            dma((2,)),
        ],
        compiler_params=pltpu.CompilerParams(
            collective_id=0, has_side_effects=True, vmem_limit_bytes=60 * 2**20
        ),
    )(positions.reshape(2, HD), queries, keys, values)
    stream = residual[0] + attended.astype(f32)
    inv = lax.rsqrt(jnp.mean(stream * stream, axis=1, keepdims=True) + 1e-05)
    normed = (stream * inv * gain).astype(bf16)
    return (stream[None], normed[None])


def solution(mesh):
    both = ("outer", "inner")
    return jax.shard_map(
        per_device,
        mesh=mesh,
        in_specs=(P(both, "head"), P(both, "head"), P(both, "head"), P(both), P(both, "head", None), P()),
        out_specs=(P(both, "head", None), P(both, "head", None)),
        check_vma=False,
    )
```
